128 devices in a mesh: section: 2 (over core), rep: 4 (over y), fsdp: 16 (over z, x).
Axes of the slice: x: 4, y: 4, z: 4, core: 2. Of those that a mesh axis runs over, the one named last changes fastest.
Arguments:
- inputs: bfloat16 [2, 64, 128, 1024], P(None, ('rep', 'fsdp')), may hold values from -6 to 6
- out_grad: bfloat16 [2, 64, 128, 1024], P(None, ('rep', 'fsdp')), may hold values from -6 to 6
- mixer_norm_gain: bfloat16 [2, 1024], P('section', 'fsdp'), may hold values from 0.5 to 1.5
- w_query: bfloat16 [2, 1024, 1024], P('section', 'fsdp'), may hold values from -0.1875 to 0.1875
- w_key: bfloat16 [2, 1024, 1024], P('section', 'fsdp'), may hold values from -0.1875 to 0.1875
- w_value: bfloat16 [2, 1024, 2048], P('section', 'fsdp'), may hold values from -0.1875 to 0.1875
- w_gate: bfloat16 [2, 1024, 2048], P('section', 'fsdp'), may hold values from -0.1875 to 0.1875
- w_alpha: bfloat16 [2, 1024, 8], P('section', 'fsdp'), may hold values from -0.1875 to 0.1875
- w_beta: bfloat16 [2, 1024, 8], P('section', 'fsdp'), may hold values from -0.1875 to 0.1875
- log_rate: float32 [2, 8], P('section'), may hold values from -1.5 to 2.5
- dt_bias: float32 [2, 8], P('section'), may hold values from -6 to -2
- conv_query: bfloat16 [2, 4, 1024], P('section', None, 'fsdp'), may hold values from -3 to 3
- conv_key: bfloat16 [2, 4, 1024], P('section', None, 'fsdp'), may hold values from -3 to 3
- conv_value: bfloat16 [2, 4, 2048], P('section', None, 'fsdp'), may hold values from -3 to 3
- out_gain: bfloat16 [2, 256], P('section', 'fsdp'), may hold values from 0.5 to 1.5
- w_out: bfloat16 [2, 2048, 1024], P('section', 'fsdp'), may hold values from -0.25 to 0.25
- gain_ffn: bfloat16 [2, 1024], P('section', 'fsdp'), may hold values from 0.5 to 1.5
- w_ffgate: bfloat16 [2, 1024, 2816], P('section', 'fsdp'), may hold values from -0.1875 to 0.1875
- w_ffup: bfloat16 [2, 1024, 2816], P('section', 'fsdp'), may hold values from -0.1875 to 0.1875
- w_ffdown: bfloat16 [2, 2816, 1024], P('section', 'fsdp'), may hold values from -0.109375 to 0.109375
Outputs:
- edges: float32 [2, 2, 64, 128, 1024], P('section', None, ('rep', 'fsdp'))
- grad_gain_mix: float32 [2, 1024], P('section', 'fsdp')
- grad_w_query: float32 [2, 1024, 1024], P('section', 'fsdp')
- grad_w_key: float32 [2, 1024, 1024], P('section', 'fsdp')
- grad_w_value: float32 [2, 1024, 2048], P('section', 'fsdp')
- grad_w_gate: float32 [2, 1024, 2048], P('section', 'fsdp')
- grad_w_alpha: float32 [2, 1024, 8], P('section', 'fsdp')
- grad_w_beta: float32 [2, 1024, 8], P('section', 'fsdp')
- grad_log_rate: float32 [2, 8], P('section')
- grad_dt_bias: float32 [2, 8], P('section')
- grad_conv_query: float32 [2, 4, 1024], P('section', None, 'fsdp')
- grad_conv_key: float32 [2, 4, 1024], P('section', None, 'fsdp')
- grad_conv_value: float32 [2, 4, 2048], P('section', None, 'fsdp')
- grad_out_gain: float32 [2, 256], P('section', 'fsdp')
- grad_w_out: float32 [2, 2048, 1024], P('section', 'fsdp')
- grad_gain_ffn: float32 [2, 1024], P('section', 'fsdp')
- grad_w_ffgate: float32 [2, 1024, 2816], P('section', 'fsdp')
- grad_w_ffup: float32 [2, 1024, 2816], P('section', 'fsdp')
- grad_w_ffdown: float32 [2, 2816, 1024], P('section', 'fsdp')
The draws below stay inside these ranges and needn't reach their ends.
All inputs are finite; a program needn't handle non-finite values.
Results may differ from the reference program's by a relative error of at most 0.033.
Values may be sent and summed in bfloat16 or wider, within the bound.
No kernel may reach another device: no remote copies, remote signals or barrier semaphores. Data moves between devices by JAX's collectives and lax.ppermute only.
A program may use at most 320 MiB of HBM per device.

```python
import jax
import jax.numpy as jnp
from jax import lax

D = 1024
H = 8
DK = 128
DV = 256
FF = 2816
KW = 4
SEQ_LEN = 128
MICRO = 2
SEQS = 64
N_SECTION = 2
N_REP = 4
N_FSDP = 16


def block_levels(rng, extent, cuts, least, high):
    level, own = 1.0, jax.random.fold_in(rng, 6)
    for dim, blocks in cuts:
        steps = jnp.exp(jax.random.uniform(jax.random.fold_in(own, dim), (blocks,), jnp.float32, least / len(cuts), high / len(cuts)))
        level = level * jnp.repeat(steps, extent[dim] // blocks).reshape([-1 if axis == dim else 1 for axis in range(len(extent))])
    return level


def bell_draw(rng, shape, width, reach, cuts=(), dtype=jnp.bfloat16):
    factor_of = block_levels(rng, shape, cuts, -0.22, 0.18) if cuts else 1.0
    entries = jax.random.normal(rng, shape, jnp.float32) * width * factor_of
    return jnp.minimum(jnp.maximum(entries, -reach), reach).astype(dtype)


def setup_inputs(seed: int = 0) -> dict:
    keys = jax.random.split(jax.random.key(seed), 21)
    return {
        "inputs": bell_draw(keys[0], (MICRO, SEQS, SEQ_LEN, D), 1.0, 6.0, ((1, 64),)),
        "out_grad": bell_draw(keys[1], (MICRO, SEQS, SEQ_LEN, D), 1.0, 6.0, ((1, 64),)),
        "mixer_norm_gain": jnp.clip(1.0 + 0.1 * jax.random.normal(keys[2], (N_SECTION, D), jnp.float32), 0.5, 1.5).astype(jnp.bfloat16),
        "w_query": bell_draw(keys[3], (N_SECTION, D, H * DK), D ** -0.5, 0.1875, ((0, 2), (1, 16))),
        "w_key": bell_draw(keys[4], (N_SECTION, D, H * DK), D ** -0.5, 0.1875, ((0, 2), (1, 16))),
        "w_value": bell_draw(keys[5], (N_SECTION, D, H * DV), D ** -0.5, 0.1875, ((0, 2), (1, 16))),
        "w_gate": bell_draw(keys[6], (N_SECTION, D, H * DV), D ** -0.5, 0.1875, ((0, 2), (1, 16))),
        "w_alpha": bell_draw(keys[7], (N_SECTION, D, H), D ** -0.5, 0.1875, ((0, 2), (1, 16))),
        "w_beta": bell_draw(keys[8], (N_SECTION, D, H), D ** -0.5, 0.1875, ((0, 2), (1, 16))),
        "log_rate": jnp.clip(-1.5 + 4.0 * jax.random.uniform(keys[9], (N_SECTION, H), jnp.float32) ** block_levels(keys[9], (N_SECTION, H), ((0, 2),), -0.2, 0.2), -1.5, 2.5),
        "dt_bias": jnp.clip(-6.0 + 4.0 * jax.random.uniform(keys[10], (N_SECTION, H), jnp.float32) ** block_levels(keys[10], (N_SECTION, H), ((0, 2),), -0.2, 0.2), -6.0, -2.0),
        "conv_query": bell_draw(keys[11], (N_SECTION, KW, H * DK), KW ** -0.5, 3.0, ((0, 2), (2, 16))),
        "conv_key": bell_draw(keys[12], (N_SECTION, KW, H * DK), KW ** -0.5, 3.0, ((0, 2), (2, 16))),
        "conv_value": bell_draw(keys[13], (N_SECTION, KW, H * DV), KW ** -0.5, 3.0, ((0, 2), (2, 16))),
        "out_gain": jnp.clip(1.0 + 0.1 * jax.random.normal(keys[14], (N_SECTION, DV), jnp.float32), 0.5, 1.5).astype(jnp.bfloat16),
        "w_out": bell_draw(keys[15], (N_SECTION, H * DV, D), (H * DV // 4) ** -0.5, 0.25, ((0, 2), (1, 16))),
        "gain_ffn": jnp.clip(1.0 + 0.1 * jax.random.normal(keys[16], (N_SECTION, D), jnp.float32), 0.5, 1.5).astype(jnp.bfloat16),
        "w_ffgate": bell_draw(keys[17], (N_SECTION, D, FF), D ** -0.5, 0.1875, ((0, 2), (1, 16))),
        "w_ffup": bell_draw(keys[18], (N_SECTION, D, FF), D ** -0.5, 0.1875, ((0, 2), (1, 16))),
        "w_ffdown": bell_draw(keys[19], (N_SECTION, FF, D), FF ** -0.5, 0.109375, ((0, 2), (1, 16))),
    }


@jax.custom_vjp
def low(v):
    return lax.optimization_barrier(v.astype(jnp.bfloat16)).astype(jnp.float32)

@jax.custom_vjp
def low_back(v):
    return v

def low_keep(v):
    return (low(v), None)

def low_pass(kept, grad):
    return (grad,)

def back_keep(v):
    return (v, None)

def back_low(kept, grad):
    return (low(grad),)
low.defvjp(low_keep, low_pass)
low_back.defvjp(back_keep, back_low)

def product(left, right):
    return jnp.dot(left, right, precision=lax.Precision.HIGHEST, preferred_element_type=jnp.float32)

def root_norm(tensor, epsilon):
    return tensor * lax.rsqrt(lax.optimization_barrier(jnp.mean(tensor * tensor, axis=-1, keepdims=True)) + epsilon)

def unit_rows(tensor):
    return tensor * lax.rsqrt(lax.optimization_barrier(jnp.sum(tensor * tensor, axis=-1, keepdims=True)) + 1e-06)

def causal_conv(values, kernel):
    taps = kernel.shape[0]
    length = values.shape[1]
    padded = jnp.pad(values, ((0, 0), (taps - 1, 0), (0, 0)))
    summed = jnp.zeros_like(values)
    for offset in range(taps):
        summed = summed + kernel[offset] * padded[:, offset:offset + length]
    return jax.nn.silu(summed)

def delta_sequence(pieces):
    queries, keys_in, values_in, strength, decay = pieces
    head_count, key_size = (keys_in.shape[1], keys_in.shape[2])
    value_size = values_in.shape[2]

    def advance(memory_state, item):
        single_query_row, single_key_row, value_row, strength_row, decay_row = item
        memory_state = memory_state * jnp.exp(decay_row)[:, None, None]
        predicted_values = jnp.einsum('pxf,px->pf', memory_state, single_key_row, precision=lax.Precision.HIGHEST)
        delta_update = strength_row[:, None] * (value_row - predicted_values)
        memory_state = memory_state + jnp.einsum('lz,lp->lzp', single_key_row, delta_update, precision=lax.Precision.HIGHEST)
        mixer_output = jnp.einsum('pxf,px->pf', memory_state, single_query_row, precision=lax.Precision.HIGHEST)
        return (memory_state, mixer_output)
    initial = jnp.zeros((head_count, key_size, value_size), jnp.float32)
    _, outputs = lax.scan(advance, initial, (queries, keys_in, values_in, strength, decay))
    return outputs

def mixer_core(projected, kernels, log_rate, dt_bias, out_gain):
    query_pre, key_pre, value_pre, gate_pre, alpha_pre, beta_pre = projected
    head_count = log_rate.shape[0]
    sequences, length = (query_pre.shape[0], query_pre.shape[1])
    queries = causal_conv(query_pre, kernels[0]).reshape(sequences, length, head_count, -1)
    keys_in = causal_conv(key_pre, kernels[1]).reshape(sequences, length, head_count, -1)
    values_in = causal_conv(value_pre, kernels[2]).reshape(sequences, length, head_count, -1)
    key_size = queries.shape[-1]
    queries = unit_rows(queries) * key_size ** (-0.5)
    keys_in = unit_rows(keys_in)
    strength = jax.nn.sigmoid(beta_pre)
    decay = -jnp.exp(log_rate) * jax.nn.softplus(alpha_pre + dt_bias)
    recur = lax.map(jax.checkpoint(delta_sequence), (queries, keys_in, values_in, strength, decay))
    gates = jax.nn.silu(gate_pre.reshape(sequences, length, head_count, -1))
    normed = root_norm(recur, 0.002) * out_gain * gates
    return normed.reshape(sequences, length, -1)

def layer(source, params):
    mixer_norm_gain, w_query, w_key, w_value, w_gate, w_alpha, w_beta, log_rate, dt_bias, conv_query, conv_key, conv_value, out_gain, w_out, gain_ffn, w_ffgate, w_ffup, w_ffdown = params
    sequences, length, model_width = source.shape
    token_rows = source.reshape(sequences * length, model_width)
    normed = low(root_norm(token_rows, 1e-06) * mixer_norm_gain)
    projected = [low_back(product(normed, matrix)).reshape(sequences, length, -1) for matrix in (w_query, w_key, w_value, w_gate, w_alpha, w_beta)]
    mixed = mixer_core(projected, (conv_query, conv_key, conv_value), log_rate, dt_bias, out_gain)
    mixed = low(mixed.reshape(sequences * length, -1))
    after_mix = token_rows + low_back(product(mixed, w_out))
    normed_ffn = low(root_norm(after_mix, 1e-06) * gain_ffn)
    gate_act = low_back(product(normed_ffn, w_ffgate))
    up_act = low_back(product(normed_ffn, w_ffup))
    hidden = low(jax.nn.silu(gate_act) * up_act)
    layer_out = after_mix + low_back(product(hidden, w_ffdown))
    return layer_out.reshape(sequences, length, model_width)

def forward(params, blocks):
    first = tuple((tensor[0] for tensor in params))
    second = tuple((tensor[1] for tensor in params))

    def one_block(block):
        middle = low_back(low(layer(block, first)))
        return layer(middle, second)
    return lax.map(jax.checkpoint(one_block), blocks)

def reference(inputs, out_grad, mixer_norm_gain, w_query, w_key, w_value, w_gate, w_alpha, w_beta, log_rate, dt_bias, conv_query, conv_key, conv_value, out_gain, w_out, gain_ffn, w_ffgate, w_ffup, w_ffdown):
    params = tuple((tensor.astype(jnp.float32) for tensor in (mixer_norm_gain, w_query, w_key, w_value, w_gate, w_alpha, w_beta, log_rate, dt_bias, conv_query, conv_key, conv_value, out_gain, w_out, gain_ffn, w_ffgate, w_ffup, w_ffdown)))
    blocks = inputs.astype(jnp.float32).reshape(MICRO * N_REP, N_FSDP, SEQ_LEN, D)
    cotangent = out_grad.astype(jnp.float32).reshape(MICRO * N_REP, N_FSDP, SEQ_LEN, D)
    block_out, pullback = jax.vjp(forward, params, blocks)
    grads, input_grad = pullback(cotangent)
    edges = jnp.stack([input_grad.reshape(MICRO, SEQS, SEQ_LEN, D), block_out.reshape(MICRO, SEQS, SEQ_LEN, D)])
    return (edges, grads[0], grads[1], grads[2], grads[3], grads[4], grads[5], grads[6], grads[7], grads[8], grads[9], grads[10], grads[11], grads[12], grads[13], grads[14], grads[15], grads[16], grads[17])
```

```python
import functools

import jax
import jax.numpy as jnp
from jax import lax
from jax.experimental import pallas as pl
from jax.experimental.pallas import tpu as pltpu
from jax.sharding import PartitionSpec as P

F32 = jnp.float32
BF16 = jnp.bfloat16
PAD = 128
LANES = 128
VMEM_LIMIT = 56 * 1024 * 1024


def mm(left, right, left_dim=1, right_dim=0):
    return lax.dot_general(
        left.astype(BF16),
        right.astype(BF16),
        (((left_dim,), (right_dim,)), ((), ())),
        preferred_element_type=F32,
    )


def halves(value):
    high = value.astype(BF16)
    return high, (value - high.astype(F32)).astype(BF16)


def mm_fine(left, right):
    left_high, left_low = halves(left)
    right_high, right_low = halves(right)
    return mm(left_high, right_high) + (mm(left_high, right_low) + mm(left_low, right_high))


def mm_ones(ones, value):
    high = value.astype(BF16)
    rest = value - high.astype(F32)
    middle = rest.astype(BF16)
    low = (rest - middle.astype(F32)).astype(BF16)
    return mm(ones, high) + (mm(ones, middle) + mm(ones, low))


def grids(length):
    rows = lax.broadcasted_iota(jnp.int32, (length, length), 0)
    cols = lax.broadcasted_iota(jnp.int32, (length, length), 1)
    return rows, cols


def lower_inverse(strict_part, rows, cols):
    length = strict_part.shape[0]
    unit = (rows == cols).astype(F32)
    base = 8
    nil = jnp.where(rows // base == cols // base, strict_part, 0.0)
    square = mm_fine(nil, nil)
    inverse = unit - nil
    inverse = inverse + mm_fine(inverse, square)
    inverse = inverse + mm_fine(inverse, mm_fine(square, square))
    size = base
    while size < length:
        joined = (rows // (2 * size) == cols // (2 * size)) & (rows // size != cols // size)
        corner = jnp.where(joined, strict_part, 0.0)
        inverse = inverse - mm_fine(inverse, mm_fine(corner, inverse))
        size *= 2
    return inverse


def shift_down(value, by):
    if by == 0:
        return value
    rows = lax.broadcasted_iota(jnp.int32, value.shape, 0)
    return jnp.where(rows >= by, pltpu.roll(value, by, 0), 0.0)


def shift_up(value, by):
    if by == 0:
        return value
    length = value.shape[0]
    rows = lax.broadcasted_iota(jnp.int32, value.shape, 0)
    return jnp.where(rows < length - by, pltpu.roll(value, length - by, 0), 0.0)


def conv_forward(value, taps):
    count = len(taps)
    total = taps[count - 1] * value
    for j in range(count - 1):
        total = total + taps[j] * shift_down(value, count - 1 - j)
    return total


def conv_backward(value, taps, grad):
    count = len(taps)
    grad_value = taps[count - 1] * grad
    grad_taps = []
    for j in range(count):
        by = count - 1 - j
        if by:
            grad_value = grad_value + taps[j] * shift_up(grad, by)
        grad_taps.append(jnp.sum(grad * shift_down(value, by), axis=0, keepdims=True))
    return grad_value, grad_taps


def silu_slope(value, gate):
    return gate * (1.0 + value * (1.0 - gate))


def pick_lane(block, lane):
    lanes = lax.broadcasted_iota(jnp.int32, block.shape, 1)
    return jnp.sum(jnp.where(lanes == lane, block, 0.0), axis=1, keepdims=True)


def softplus(value):
    return jnp.maximum(value, 0.0) + jnp.log1p(jnp.exp(-jnp.abs(value)))


def head_states(query_pre, key_pre, value_pre, alpha, beta, taps, rate, bias, masks):
    rows, cols, lower, strict = masks
    key_size = query_pre.shape[-1]
    query_conv = conv_forward(query_pre, taps[0])
    key_conv = conv_forward(key_pre, taps[1])
    value_conv = conv_forward(value_pre, taps[2])
    query_gate = jax.nn.sigmoid(query_conv)
    key_gate = jax.nn.sigmoid(key_conv)
    value_gate = jax.nn.sigmoid(value_conv)
    query_act = query_conv * query_gate
    key_act = key_conv * key_gate
    values = value_conv * value_gate
    query_scale = lax.rsqrt(jnp.sum(query_act * query_act, axis=-1, keepdims=True) + 1e-06)
    key_scale = lax.rsqrt(jnp.sum(key_act * key_act, axis=-1, keepdims=True) + 1e-06)
    query_unit = query_act * query_scale
    keys = key_act * key_scale
    queries = query_unit * key_size ** (-0.5)
    strength = jax.nn.sigmoid(beta)
    decay = -rate * softplus(alpha + bias)
    running = mm_ones(lower.astype(BF16), jnp.broadcast_to(decay, rows.shape))
    spread = running - running.T
    ratios = jnp.exp(jnp.where(lower, spread, 0.0)) * lower.astype(F32)
    key_key = mm(keys, keys, 1, 1)
    query_key = mm(queries, keys, 1, 1)
    key_ratio = jnp.where(strict, key_key * ratios, 0.0)
    weighting = query_key * ratios
    return dict(
        query_conv=query_conv,
        key_conv=key_conv,
        value_conv=value_conv,
        query_gate=query_gate,
        key_gate=key_gate,
        value_gate=value_gate,
        query_scale=query_scale,
        key_scale=key_scale,
        query_unit=query_unit,
        queries=queries,
        keys=keys,
        values=values,
        strength=strength,
        decay=decay,
        ratios=ratios,
        key_ratio=key_ratio,
        weighting=weighting,
    )


def read_taps(ref, lo, hi):
    return [ref[j : j + 1, lo:hi] for j in range(4)]


def mixer_forward_kernel(
    heads, length, query_ref, key_ref, value_ref, gate_ref, ab_ref, tq_ref, tk_ref, tv_ref, head_ref, gain_ref, mixed_ref, inverse_ref
):
    step = pl.program_id(0)
    per_step = inverse_ref.shape[0]
    sequences = query_ref.shape[0] // length
    key_size = query_ref.shape[1] // per_step
    value_size = value_ref.shape[1] // per_step
    rows, cols = grids(length)
    masks = (rows, cols, rows >= cols, rows > cols)
    gain = gain_ref[0:1, :]
    for local in range(per_step):
        head = step * per_step + local
        kc = slice(local * key_size, (local + 1) * key_size)
        vc = slice(local * value_size, (local + 1) * value_size)
        rate = jnp.exp(pick_lane(head_ref[0:1, :], head))
        bias = pick_lane(head_ref[1:2, :], head)
        taps = (
            read_taps(tq_ref, kc.start, kc.stop),
            read_taps(tk_ref, kc.start, kc.stop),
            read_taps(tv_ref, vc.start, vc.stop),
        )
        for seq in range(sequences):
            tr = slice(seq * length, (seq + 1) * length)
            ab = ab_ref[tr, :]
            alpha = pick_lane(ab, head)
            beta = pick_lane(ab, heads + head)
            s = head_states(
                query_ref[tr, kc], key_ref[tr, kc], value_ref[tr, vc], alpha, beta, taps, rate, bias, masks
            )
            inverse = lower_inverse(s["strength"] * s["key_ratio"], rows, cols)
            inverse_ref[local, seq] = inverse
            updates = mm(inverse, s["strength"] * s["values"])
            recur = mm(s["weighting"], updates)
            scale = lax.rsqrt(jnp.mean(recur * recur, axis=-1, keepdims=True) + 0.002)
            gate = gate_ref[tr, vc]
            mixed = recur * scale * gain * (gate * jax.nn.sigmoid(gate))
            mixed_ref[tr, vc] = mixed.astype(mixed_ref.dtype)


def mixer_backward_kernel(
    heads,
    length,
    query_ref,
    key_ref,
    value_ref,
    gate_ref,
    ab_ref,
    tq_ref,
    tk_ref,
    tv_ref,
    head_ref,
    gain_ref,
    inverse_ref,
    grad_ref,
    pre_a_ref,
    pre_b_ref,
    gtq_ref,
    gtk_ref,
    gtv_ref,
    ghead_ref,
    ggain_ref,
    gab_ref,
):
    step = pl.program_id(0)
    per_step = inverse_ref.shape[0]
    sequences = query_ref.shape[0] // length
    key_size = query_ref.shape[1] // per_step
    value_size = value_ref.shape[1] // per_step
    key_cols = heads * key_size
    value_cols = heads * value_size
    rows, cols = grids(length)
    lower, strict = rows >= cols, rows > cols
    masks = (rows, cols, lower, strict)
    upper = (rows <= cols).astype(BF16)
    gain = gain_ref[0:1, :]

    @pl.when(step == 0)
    def _():
        ghead_ref[...] = jnp.zeros_like(ghead_ref)
        ggain_ref[...] = jnp.zeros_like(ggain_ref)
        gab_ref[...] = jnp.zeros_like(gab_ref)

    lanes = lax.broadcasted_iota(jnp.int32, (length, LANES), 1)
    lane_row = lax.broadcasted_iota(jnp.int32, (1, LANES), 1)
    for local in range(per_step):
        head = step * per_step + local
        kc = slice(local * key_size, (local + 1) * key_size)
        vc = slice(local * value_size, (local + 1) * value_size)
        rate = jnp.exp(pick_lane(head_ref[0:1, :], head))
        bias = pick_lane(head_ref[1:2, :], head)
        taps = (
            read_taps(tq_ref, kc.start, kc.stop),
            read_taps(tk_ref, kc.start, kc.stop),
            read_taps(tv_ref, vc.start, vc.stop),
        )
        tap_totals = None
        gain_total = None
        rate_total = None
        bias_total = None
        for seq in range(sequences):
            tr = slice(seq * length, (seq + 1) * length)
            ab = ab_ref[tr, :]
            alpha = pick_lane(ab, head)
            beta = pick_lane(ab, heads + head)
            query_pre, key_pre, value_pre = query_ref[tr, kc], key_ref[tr, kc], value_ref[tr, vc]
            s = head_states(query_pre, key_pre, value_pre, alpha, beta, taps, rate, bias, masks)
            strength, keys, queries, values = s["strength"], s["keys"], s["queries"], s["values"]
            inverse = inverse_ref[local, seq]
            updates = mm(inverse, strength * values)
            recur = mm(s["weighting"], updates)
            scale = lax.rsqrt(jnp.mean(recur * recur, axis=-1, keepdims=True) + 0.002)
            normal = recur * scale
            gate = gate_ref[tr, vc]
            gate_sig = jax.nn.sigmoid(gate)
            gate_act = gate * gate_sig
            grad = grad_ref[tr, vc]
            grad_normal = grad * normal
            gain_part = jnp.sum(grad_normal * gate_act, axis=0, keepdims=True)
            grad_gate = grad_normal * gain * silu_slope(gate, gate_sig)
            grad_norm = grad * gain * gate_act
            grad_recur = scale * (grad_norm - normal * jnp.mean(grad_norm * normal, axis=-1, keepdims=True))
            grad_weight = jnp.where(lower, mm(grad_recur, updates, 1, 1), 0.0)
            grad_updates = mm(s["weighting"], grad_recur, 0, 0)
            grad_target = mm(inverse, grad_updates, 0, 0)
            grad_values = strength * grad_target
            grad_system = jnp.where(strict, -mm(grad_target, updates, 1, 1), 0.0)
            ratio_part = grad_system * s["key_ratio"]
            grad_strength = jnp.sum(grad_target * values, axis=-1, keepdims=True) + jnp.sum(
                ratio_part, axis=-1, keepdims=True
            )
            grad_kk = grad_system * strength * s["ratios"]
            grad_qk = grad_weight * s["ratios"]
            through = jnp.where(strict, ratio_part * strength + grad_weight * s["weighting"], 0.0)
            grad_running = jnp.sum(through - through.T, axis=-1, keepdims=True)
            grad_decay = mm_ones(upper, jnp.broadcast_to(grad_running, rows.shape))[:, 0:1]
            grad_keys = mm(grad_kk + grad_kk.T, keys) + mm(grad_qk, queries, 0, 0)
            grad_queries = mm(grad_qk, keys) * key_size ** (-0.5)
            query_unit = s["query_unit"]
            grad_query_act = s["query_scale"] * (
                grad_queries - query_unit * jnp.sum(grad_queries * query_unit, axis=-1, keepdims=True)
            )
            grad_key_act = s["key_scale"] * (
                grad_keys - keys * jnp.sum(grad_keys * keys, axis=-1, keepdims=True)
            )
            grad_query_pre, query_taps = conv_backward(
                query_pre, taps[0], grad_query_act * silu_slope(s["query_conv"], s["query_gate"])
            )
            grad_key_pre, key_taps = conv_backward(
                key_pre, taps[1], grad_key_act * silu_slope(s["key_conv"], s["key_gate"])
            )
            grad_value_pre, value_taps = conv_backward(
                value_pre, taps[2], grad_values * silu_slope(s["value_conv"], s["value_gate"])
            )
            grad_beta = grad_strength * strength * (1.0 - strength)
            grad_inner = -rate * grad_decay * jax.nn.sigmoid(alpha + bias)
            rate_part = jnp.sum(grad_decay * s["decay"], axis=0, keepdims=True)
            bias_part = jnp.sum(grad_inner, axis=0, keepdims=True)

            def put(ref, first, block):
                start = pl.multiple_of(first, LANES)
                ref[tr, pl.ds(start, block.shape[1])] = block.astype(ref.dtype)

            put(pre_a_ref, value_cols + head * key_size, grad_query_pre)
            put(pre_b_ref, value_cols + head * key_size, grad_key_pre)
            put(pre_a_ref, head * value_size, grad_value_pre)
            put(pre_b_ref, head * value_size, grad_gate)
            gab_ref[tr, :] = gab_ref[tr, :] + (
                jnp.where(lanes == head, grad_inner, 0.0) + jnp.where(lanes == heads + head, grad_beta, 0.0)
            )
            parts = (query_taps, key_taps, value_taps)
            if tap_totals is None:
                tap_totals, gain_total, rate_total, bias_total = parts, gain_part, rate_part, bias_part
            else:
                tap_totals = tuple(
                    [a + b for a, b in zip(one, two)] for one, two in zip(tap_totals, parts)
                )
                gain_total = gain_total + gain_part
                rate_total = rate_total + rate_part
                bias_total = bias_total + bias_part
        for j in range(4):
            gtq_ref[j : j + 1, kc] = tap_totals[0][j]
            gtk_ref[j : j + 1, kc] = tap_totals[1][j]
            gtv_ref[j : j + 1, vc] = tap_totals[2][j]
        ggain_ref[0:1, :] = ggain_ref[0:1, :] + gain_total
        ghead_ref[0:1, :] = ghead_ref[0:1, :] + jnp.where(lane_row == head, rate_total, 0.0)
        ghead_ref[1:2, :] = ghead_ref[1:2, :] + jnp.where(lane_row == head, bias_total, 0.0)

    @pl.when(step == heads // per_step - 1)
    def _():
        first = key_cols + value_cols
        pre_a_ref[:, first : first + LANES] = gab_ref[...].astype(pre_a_ref.dtype)


HEADS_PER_STEP = 2


def mixer_specs(tokens, heads, key_size, value_size):
    per_step = HEADS_PER_STEP
    wide_key, wide_value = per_step * key_size, per_step * value_size
    key_first = heads * value_size // wide_key
    ab_first = (heads * value_size + heads * key_size) // LANES
    return [
        pl.BlockSpec((tokens, wide_key), lambda h: (0, key_first + h)),
        pl.BlockSpec((tokens, wide_key), lambda h: (0, key_first + h)),
        pl.BlockSpec((tokens, wide_value), lambda h: (0, h)),
        pl.BlockSpec((tokens, wide_value), lambda h: (0, h)),
        pl.BlockSpec((tokens, LANES), lambda h: (0, ab_first)),
        pl.BlockSpec((8, wide_key), lambda h: (0, h)),
        pl.BlockSpec((8, wide_key), lambda h: (0, h)),
        pl.BlockSpec((8, wide_value), lambda h: (0, h)),
        pl.BlockSpec((8, LANES), lambda h: (0, 0)),
        pl.BlockSpec((8, value_size), lambda h: (0, 0)),
    ]


def mixer_forward(pre_a, pre_b, small, length, heads, key_size, value_size):
    tokens = pre_a.shape[0]
    per_step = HEADS_PER_STEP
    return pl.pallas_call(
        functools.partial(mixer_forward_kernel, heads, length),
        grid=(heads // per_step,),
        in_specs=mixer_specs(tokens, heads, key_size, value_size),
        out_specs=[
            pl.BlockSpec((tokens, per_step * value_size), lambda h: (0, h)),
            pl.BlockSpec((per_step, tokens // length, length, length), lambda h: (h, 0, 0, 0)),
        ],
        out_shape=[
            jax.ShapeDtypeStruct((tokens, heads * value_size), BF16),
            jax.ShapeDtypeStruct((heads, tokens // length, length, length), F32),
        ],
        compiler_params=pltpu.CompilerParams(vmem_limit_bytes=VMEM_LIMIT),
        name="mixer_forward",
    )(pre_a, pre_b, pre_a, pre_b, pre_a, *small)


def mixer_backward(pre_a, pre_b, small, inverse, grad, length, heads, key_size, value_size):
    tokens, width_a = pre_a.shape
    width_b = pre_b.shape[1]
    per_step = HEADS_PER_STEP
    wide_key, wide_value = per_step * key_size, per_step * value_size
    fixed = lambda h: (0, 0)
    moving = lambda h: (0, h)
    return pl.pallas_call(
        functools.partial(mixer_backward_kernel, heads, length),
        grid=(heads // per_step,),
        in_specs=mixer_specs(tokens, heads, key_size, value_size)
        + [
            pl.BlockSpec((per_step, tokens // length, length, length), lambda h: (h, 0, 0, 0)),
            pl.BlockSpec((tokens, wide_value), moving),
        ],
        out_specs=[
            pl.BlockSpec((tokens, width_a), fixed),
            pl.BlockSpec((tokens, width_b), fixed),
            pl.BlockSpec((8, wide_key), moving),
            pl.BlockSpec((8, wide_key), moving),
            pl.BlockSpec((8, wide_value), moving),
            pl.BlockSpec((8, LANES), fixed),
            pl.BlockSpec((8, value_size), fixed),
        ],
        out_shape=[
            jax.ShapeDtypeStruct((tokens, width_a), BF16),
            jax.ShapeDtypeStruct((tokens, width_b), BF16),
            jax.ShapeDtypeStruct((8, heads * key_size), F32),
            jax.ShapeDtypeStruct((8, heads * key_size), F32),
            jax.ShapeDtypeStruct((8, heads * value_size), F32),
            jax.ShapeDtypeStruct((8, LANES), F32),
            jax.ShapeDtypeStruct((8, value_size), F32),
        ],
        scratch_shapes=[pltpu.VMEM((tokens, LANES), F32)],
        compiler_params=pltpu.CompilerParams(vmem_limit_bytes=VMEM_LIMIT),
        name="mixer_backward",
    )(pre_a, pre_b, pre_a, pre_b, pre_a, *small, inverse, grad)


def swapped(value):
    return lax.ppermute(value, "section", [(0, 1), (1, 0)])


def pair_sum(value):
    return value + swapped(value)


SIDE = 4


class Ring:
    def __init__(self, axis):
        if axis == "y":
            self.name, self.position = "rep", lax.axis_index("rep")
            self.pairs = lambda by: [(y, (y + by) % SIDE) for y in range(SIDE)]
            return
        self.name = "fsdp"
        index = lax.axis_index("fsdp")
        z, x = index // SIDE, index % SIDE
        if axis == "x":
            self.position = x
            step = lambda z, x, by: z * SIDE + (x + by) % SIDE
        else:
            self.position = z
            step = lambda z, x, by: (z + by) % SIDE * SIDE + x
        self.pairs = lambda by: [
            (z * SIDE + x, step(z, x, by)) for z in range(SIDE) for x in range(SIDE)
        ]

    def move(self, value, by):
        return lax.ppermute(value, self.name, self.pairs(by))


def ring_gather(block, ring):
    count = block.shape[0] // 2
    from_left = ring.move(block, 1)
    from_right = ring.move(block, -1)
    far_first = ring.move(from_left[:count], 1)
    far_last = ring.move(from_right[count:], -1)
    return block, from_right, far_first, far_last, from_left


def torus_gather(shard, x_first):
    rows = shard.shape[0]
    if x_first:
        block = jnp.concatenate(ring_gather(shard, Ring("x")), axis=0)
        pieces = ring_gather(block, Ring("z"))
        return jnp.concatenate(pieces, axis=0), pieces[1]
    block = jnp.concatenate(ring_gather(shard, Ring("z")), axis=0)
    own, right, far_first, far_last, left = ring_gather(block, Ring("x"))
    cut = lambda piece, k: piece[k * rows : (k + 1) * rows]
    rows_of = []
    for kz in range(SIDE):
        far = cut(far_first, kz) if kz < SIDE // 2 else cut(far_last, kz - SIDE // 2)
        rows_of += [cut(own, kz), cut(right, kz), far, cut(left, kz)]
    return jnp.concatenate(rows_of, axis=0), right


def added(first, *others):
    total = first.astype(F32)
    for other in others:
        total = total + other.astype(F32)
    return total.astype(BF16)


def ring_scatter(parts, ring):
    ahead, behind, rest, own = parts
    count = own.shape[0] // 2
    from_left = ring.move(ahead, 1)
    from_right = ring.move(behind, -1)
    next_left = ring.move(added(rest[:count], from_left[:count]), 1)
    next_right = ring.move(added(rest[count:], from_right[:count]), -1)
    return jnp.concatenate(
        [
            added(own[:count], next_left, from_right[count:]),
            added(own[count:], from_left[count:], next_right),
        ],
        axis=0,
    )


def torus_scatter(chunks, x_first):
    first, second = ("x", "z") if x_first else ("z", "x")

    def parts(total, make):
        quarter, half = total // SIDE, total // SIDE // 2
        join = lambda one, two: make([(one, one + half), (two, two + half)])
        return [
            join(2 * quarter, quarter + half),
            join(2 * quarter + half, 3 * quarter),
            join(quarter, 3 * quarter + half),
            make([(0, quarter)]),
        ]

    block = ring_scatter(parts(chunks.total, chunks.make), Ring(first))
    make = lambda cuts: jnp.concatenate([block[i:j] for i, j in cuts], axis=0)
    return ring_scatter(parts(block.shape[0], make), Ring(second))


class Chunks:
    def __init__(self, products):
        self.products = products
        self.total = products[0][0].shape[1]

    def make(self, cuts):
        blocks = []
        for left, right, extra in self.products:
            rows = jnp.concatenate([left[:, i:j] for i, j in cuts], axis=1)
            block = dot_tn(rows, right)
            if extra is not None:
                block = block + jnp.concatenate([extra[i:j] for i, j in cuts], axis=0)
            blocks.append(block.astype(BF16))
        return jnp.concatenate(blocks, axis=1)


def own_order(rows):
    index = lax.axis_index("fsdp")
    z, x = index // SIDE, index % SIDE
    place = jnp.arange(SIDE * SIDE * rows, dtype=jnp.int32)
    by_z, by_x, offset = place // (SIDE * rows), place // rows % SIDE, place % rows
    source = ((z + by_z) % SIDE * SIDE + (x + by_x) % SIDE) * rows + offset
    return (place[:, None] == source[None, :]).astype(BF16)


def flipped_order(rows):
    place = jnp.arange(SIDE * SIDE * rows, dtype=jnp.int32)
    by_x, by_z, offset = place // (SIDE * rows), place // rows % SIDE, place % rows
    source = (by_z * SIDE + by_x) * rows + offset
    return (place[:, None] == source[None, :]).astype(BF16)


def rep_sum(value):
    near = [(0, 1), (1, 0), (2, 3), (3, 2)]
    across = [(0, 3), (3, 0), (1, 2), (2, 1)]
    count = value.shape[0] // 2
    done = []
    for part, order in ((value[:count], (near, across)), (value[count:], (across, near))):
        for pairs in order:
            part = added(part, lax.ppermute(part, "rep", pairs))
        done.append(part)
    return jnp.concatenate(done, axis=0)


def dot(left, right):
    return jnp.dot(left, right, preferred_element_type=F32)


def dot_nt(left, right):
    return lax.dot_general(left, right, (((1,), (1,)), ((), ())), preferred_element_type=F32)


def dot_tn(left, right):
    return lax.dot_general(left, right, (((0,), (0,)), ((), ())), preferred_element_type=F32)


def inverse_rms(value):
    return lax.rsqrt(jnp.mean(value * value, axis=-1, keepdims=True) + 1e-06)


def norm_backward(value, gain, grad):
    scale = inverse_rms(value)
    unit = value * scale
    inner = grad * gain
    grad_value = scale * (inner - unit * jnp.mean(inner * unit, axis=-1, keepdims=True))
    return grad_value, jnp.sum(grad * unit, axis=0)


def per_device(
    inputs,
    out_grad,
    mixer_norm_gain,
    w_query,
    w_key,
    w_value,
    w_gate,
    w_alpha,
    w_beta,
    log_rate,
    dt_bias,
    conv_query,
    conv_key,
    conv_value,
    out_gain,
    w_out,
    gain_ffn,
    w_ffgate,
    w_ffup,
    w_ffdown,
):
    core = lax.axis_index("section")
    first_core = core == 0
    micro, _, length, width = inputs.shape
    tokens = micro * length
    members = lax.axis_size("fsdp")
    cores = 2
    all_heads = log_rate.shape[1]
    heads = all_heads // cores
    key_size = w_query.shape[2] // all_heads
    value_size = w_value.shape[2] // all_heads
    key_cols, value_cols = heads * key_size, heads * value_size
    ffn_cols = w_ffgate.shape[2] // cores
    rows = w_query.shape[1]
    taps = conv_query.shape[1]
    out_rows, down_rows = w_out.shape[1], w_ffdown.shape[1]
    value_split = conv_value.shape[2] // rows
    gain_rows = out_gain.shape[1]

    def choose(first, second):
        return jnp.where(first_core, first, second)

    small_cols = jnp.concatenate(
        [
            mixer_norm_gain[0][:, None],
            gain_ffn[0][:, None],
            conv_query[0].T,
            conv_key[0].T,
            conv_value[0].reshape(taps * value_split, rows).T,
            jnp.pad(out_gain[0], (0, rows - gain_rows))[:, None],
        ],
        axis=1,
    )
    small_count = small_cols.shape[1]
    ab_cols = 2 * heads
    spare = PAD - ab_cols - small_count
    main_a = value_cols + key_cols
    split = 2 * LANES
    out_first, down_first = ffn_cols, ffn_cols + value_cols

    lane_rows = out_rows + down_rows
    both_t = jnp.concatenate([w_out[0].T, w_ffdown[0].T], axis=1)
    both_t = jnp.pad(both_t, ((0, 0), (0, -lane_rows % LANES))).reshape(members, rows, -1)
    both_t = lax.all_to_all(both_t, "fsdp", split_axis=0, concat_axis=0, tiled=True)
    out_t = both_t[:, :, :out_rows].transpose(1, 0, 2).reshape(rows, members * out_rows)
    down_t = both_t[:, :, out_rows:lane_rows].transpose(1, 0, 2).reshape(rows, members * down_rows)

    def cut(w, k):
        n = w.shape[1] // cores
        return w[:, k * n : (k + 1) * n]

    def in_piece(k):
        return jnp.concatenate(
            [cut(w[0], k) for w in (w_value, w_query, w_alpha, w_beta)]
            + [small_cols, jnp.zeros((rows, spare), BF16)]
            + [cut(w[0], k) for w in (w_gate, w_key)],
            axis=1,
        )

    def ffn_piece(k):
        down = cut(down_t, k)
        return jnp.concatenate(
            [cut(w_ffgate[0], k), cut(out_t, k), down[:, :split], cut(w_ffup[0], k), down[:, split:]], axis=1
        )

    def both(make):
        left, right = make(0), make(1)
        own, sent = choose(left, right), choose(right, left)
        received = swapped(sent)
        return choose(own, received), choose(received, own)

    in_pieces = both(in_piece)
    ffn_pieces = both(ffn_piece)
    in_a = main_a + PAD
    ffn_a = down_first + split
    rate_rows = jnp.stack([log_rate[0], dt_bias[0]])
    other_rates = swapped(rate_rows)
    rates = (choose(rate_rows, other_rates), choose(other_rates, rate_rows))
    order = own_order(rows)
    flip = flipped_order(rows)

    def ordered(value):
        return dot(value, order)

    def unordered(value):
        high = value.astype(BF16)
        rest = value - high.astype(F32)
        middle = rest.astype(BF16)
        low = (rest - middle.astype(F32)).astype(BF16)
        return dot_nt(high, order) + (dot_nt(middle, order) + dot_nt(low, order))

    def flipped(value):
        return dot(value, flip).astype(BF16)

    def after(value, token):
        return value if token is None else lax.optimization_barrier((value, token))[0]

    def fetch(pieces, wide, token):
        pieces = after(pieces, token)
        full_a, token_a = torus_gather(pieces[:, :wide], True)
        full_b, token_b = torus_gather(pieces[:, wide:], False)
        return full_a, full_b, (token_a, token_b)

    def small_params(in_full, layer):
        first = main_a + ab_cols
        small_own = in_full[:, first : first + small_count].T
        small = dot_nt(small_own, order)
        at = 2
        conv_q = small[at : at + taps]
        conv_k = small[at + taps : at + 2 * taps]
        at += 2 * taps
        conv_v = small[at : at + taps * value_split].reshape(taps, value_split, members, rows)
        conv_v = conv_v.transpose(0, 2, 1, 3).reshape(taps, members * value_split * rows)
        at += taps * value_split
        gain_out = small[at].reshape(members, rows)[:, :gain_rows].reshape(1, members * gain_rows)

        def own_cols(value, count):
            mine = choose(value[:, :count], value[:, count:])
            return jnp.pad(mine, ((0, 8 - value.shape[0]), (0, 0)))

        rate = own_cols(rates[layer], heads)
        smalls = (
            own_cols(conv_q, key_cols),
            own_cols(conv_k, key_cols),
            own_cols(conv_v, value_cols),
            jnp.pad(rate, ((0, 0), (0, LANES - heads))),
            jnp.pad(gain_out, ((0, 7), (0, 0))),
        )
        return small_own[0].astype(F32), small_own[1].astype(F32), smalls

    def forward_layer(source, in_full, ffn_full, params):
        in_w, in_v = in_full
        ffn_w, ffn_v = ffn_full
        gain_mix, gain_in, smalls = params
        normed = (source * inverse_rms(source) * gain_mix).astype(BF16)
        pre_a, pre_b = dot(normed, in_w), dot(normed, in_v)
        mixed, inverse = mixer_forward(pre_a, pre_b, smalls, length, heads, key_size, value_size)
        after_mix = source + pair_sum(dot_nt(mixed, ffn_w[:, out_first:down_first]))
        normed_ffn = (after_mix * inverse_rms(after_mix) * gain_in).astype(BF16)
        gate_act = dot(normed_ffn, ffn_w[:, :ffn_cols])
        up_act = dot(normed_ffn, ffn_v[:, :ffn_cols])
        hidden = (gate_act * jax.nn.sigmoid(gate_act) * up_act).astype(BF16)
        part = dot_nt(hidden[:, :split], ffn_w[:, down_first:]) + dot_nt(hidden[:, split:], ffn_v[:, ffn_cols:])
        layer_out = after_mix + pair_sum(part)
        return layer_out, (source, normed, pre_a, pre_b, inverse, mixed, after_mix, normed_ffn, gate_act, up_act, hidden)

    def backward_layer(grad_top, saved, in_full, ffn_full, params):
        source, normed, pre_a, pre_b, inverse, mixed, after_mix, normed_ffn, gate_act, up_act, hidden = saved
        in_w, in_v = in_full
        ffn_w, ffn_v = ffn_full
        gain_mix, gain_in, smalls = params
        down_grad = grad_top.astype(BF16)
        hidden_grad = jnp.concatenate(
            [dot(down_grad, ffn_w[:, down_first:]), dot(down_grad, ffn_v[:, ffn_cols:])], axis=1
        )
        gate_sig = jax.nn.sigmoid(gate_act)
        gate_grad = (hidden_grad * up_act * silu_slope(gate_act, gate_sig)).astype(BF16)
        up_grad = (hidden_grad * (gate_act * gate_sig)).astype(BF16)
        ffn_in_grad = pair_sum(dot_nt(gate_grad, ffn_w[:, :ffn_cols]) + dot_nt(up_grad, ffn_v[:, :ffn_cols]))
        residual, grad_gain_ffn = norm_backward(after_mix, gain_in, ffn_in_grad)
        mix_grad = grad_top + residual
        mix_low = mix_grad.astype(BF16)
        mixed_grad = dot(mix_low, ffn_w[:, out_first:down_first])
        grad_ffn = (
            torus_scatter(
                Chunks(
                    [
                        (flipped(normed_ffn), gate_grad, None),
                        (flipped(mix_low), mixed, None),
                        (flipped(down_grad), hidden[:, :split], None),
                    ]
                ),
                True,
            ),
            torus_scatter(Chunks([(normed_ffn, up_grad, None), (down_grad, hidden[:, split:], None)]), False),
        )
        grad_ffn = rep_sum(jnp.concatenate(grad_ffn, axis=1))
        pre_a_grad, pre_b_grad, gtq, gtk, gtv, ghead, ggain = mixer_backward(
            pre_a, pre_b, smalls, inverse, mixed_grad, length, heads, key_size, value_size
        )
        normed_grad = pair_sum(dot_nt(pre_a_grad, in_w) + dot_nt(pre_b_grad, in_v))
        source_part, grad_gain_mix = norm_backward(source, gain_mix, normed_grad)
        source_grad = mix_grad + source_part

        def whole_cols(value):
            zeros = jnp.zeros_like(value)
            return choose(
                jnp.concatenate([value, zeros], axis=1), jnp.concatenate([zeros, value], axis=1)
            )

        conv_v = whole_cols(gtv[:taps]).reshape(taps, members, value_split, rows)
        conv_v = conv_v.transpose(0, 2, 1, 3).reshape(taps * value_split, members * rows)
        gain_out = ggain[0].reshape(members, gain_rows)
        head_part = whole_cols(ghead[:2, :heads]).reshape(1, 2 * all_heads)
        head_part = jnp.broadcast_to(head_part, (members, 2 * all_heads))
        tail = jnp.concatenate(
            [gain_out, head_part, jnp.zeros((members, rows - gain_rows - 2 * all_heads), F32)], axis=1
        )
        once = first_core.astype(F32)
        gains = jnp.stack([grad_gain_mix, grad_gain_ffn]) * once
        others = jnp.concatenate(
            [whole_cols(gtq[:taps]), whole_cols(gtk[:taps]), conv_v, tail.reshape(1, members * rows)], axis=0
        )
        small = jnp.concatenate([gains.astype(BF16), ordered(others.astype(BF16)).astype(BF16)], axis=0)
        small = jnp.concatenate(
            [jnp.zeros((ab_cols, width), BF16), small, jnp.zeros((spare, width), BF16)], axis=0
        )
        small = lax.dot_general(flip, small, (((0,), (1,)), ((), ())), preferred_element_type=F32)
        turned = flipped(normed)
        grad_in = (
            torus_scatter(
                Chunks([(turned, pre_a_grad[:, :main_a], None), (turned, pre_a_grad[:, main_a:], small)]), True
            ),
            torus_scatter(Chunks([(normed, pre_b_grad, None)]), False),
        )
        grad_in = rep_sum(jnp.concatenate(grad_in, axis=1))
        return source_grad, grad_in, grad_ffn

    def to_owner(first, second):
        own = choose(first, second)
        received = swapped(choose(second, first))
        return choose(own, received), choose(received, own)

    source = ordered(inputs.reshape(tokens, width))
    in_0a, in_0b, token = fetch(in_pieces[0], in_a, None)
    ffn_0a, ffn_0b, token = fetch(ffn_pieces[0], ffn_a, token)
    in_1a, in_1b, token = fetch(in_pieces[1], in_a, token)
    ffn_1a, ffn_1b, token = fetch(ffn_pieces[1], ffn_a, token)
    in_0, ffn_0, in_1, ffn_1 = (in_0a, in_0b), (ffn_0a, ffn_0b), (in_1a, in_1b), (ffn_1a, ffn_1b)
    params_0, params_1 = small_params(in_0a, 0), small_params(in_1a, 1)
    first_out, first_saved = forward_layer(source, in_0, ffn_0, params_0)
    middle = first_out.astype(BF16).astype(F32)
    block_out, second_saved = forward_layer(middle, in_1, ffn_1, params_1)
    cotangent = ordered(out_grad.reshape(tokens, width))
    second_grad, second_in, second_ffn = backward_layer(cotangent, second_saved, in_1, ffn_1, params_1)
    input_grad, first_in, first_ffn = backward_layer(
        second_grad.astype(BF16).astype(F32), first_saved, in_0, ffn_0, params_0
    )
    in_left, in_right = to_owner(first_in, second_in)
    ffn_left, ffn_right = to_owner(first_ffn, second_ffn)

    def joined(left, right, first, count):
        span = slice(first, first + count)
        return jnp.concatenate([left[:, span], right[:, span]], axis=1).astype(F32)[None]

    gate_first = main_a + PAD
    up_first = down_first + split
    down_rest = up_first + ffn_cols
    full_out = jnp.concatenate(
        [side[:, out_first:down_first] for side in (ffn_left, ffn_right)], axis=1
    ).reshape(rows, members, out_rows)
    full_down = jnp.concatenate(
        [part for side in (ffn_left, ffn_right) for part in (side[:, down_first:up_first], side[:, down_rest:])], axis=1
    ).reshape(rows, members, down_rows)
    back = jnp.concatenate([full_out, full_down], axis=2).transpose(1, 0, 2)
    back = jnp.pad(back, ((0, 0), (0, 0), (0, -lane_rows % LANES)))
    back = lax.all_to_all(back, "fsdp", split_axis=0, concat_axis=0, tiled=True).reshape(width, -1)
    grad_out = back[:, :out_rows].T.astype(F32)
    grad_down = back[:, out_rows:lane_rows].T.astype(F32)

    first = main_a + ab_cols
    small = in_left[:, first : first + small_count].astype(F32) + in_right[:, first : first + small_count].astype(F32)
    small = small.T
    tail = small[small_count - 1]
    conv_at = 2 + 2 * taps
    head_grads = tail[gain_rows : gain_rows + 2 * all_heads].reshape(2, all_heads)
    edges = unordered(choose(input_grad, block_out)).reshape(1, micro, 1, length, width)
    return (
        edges,
        small[0][None],
        joined(in_left, in_right, value_cols, key_cols),
        joined(in_left, in_right, gate_first + value_cols, key_cols),
        joined(in_left, in_right, 0, value_cols),
        joined(in_left, in_right, gate_first, value_cols),
        joined(in_left, in_right, main_a, heads),
        joined(in_left, in_right, main_a + heads, heads),
        head_grads[0:1],
        head_grads[1:2],
        small[2 : 2 + taps][None],
        small[2 + taps : 2 + 2 * taps][None],
        small[conv_at : conv_at + taps * value_split].reshape(1, taps, value_split * rows),
        tail[:gain_rows][None],
        grad_out[None],
        small[1][None],
        joined(ffn_left, ffn_right, 0, ffn_cols),
        joined(ffn_left, ffn_right, up_first, ffn_cols),
        grad_down[None],
    )


def solution(mesh):
    across = P("section", "fsdp", None)
    lanes = P("section", None, "fsdp")
    vector = P("section", "fsdp")
    rates = P("section", None)
    tokens = P(None, ("rep", "fsdp"), None, None)
    placed = (
        (tokens, tokens, vector)
        + (across,) * 6
        + (rates, rates, lanes, lanes, lanes, vector, across, vector, across, across, across)
    )
    return jax.shard_map(
        per_device,
        mesh=mesh,
        in_specs=placed,
        out_specs=(P("section", None, ("rep", "fsdp"), None, None), vector)
        + (across,) * 6
        + (rates, rates, lanes, lanes, lanes, vector, across, vector, across, across, across),
        check_vma=False,
    )
```

```python
import functools

import jax
import jax.numpy as jnp
from jax import lax
from jax.experimental import pallas as pl
from jax.experimental.pallas import tpu as pltpu
from jax.sharding import PartitionSpec as P

F32 = jnp.float32
BF16 = jnp.bfloat16
PAD = 128
LANES = 128
VMEM_LIMIT = 56 * 1024 * 1024


def mm(left, right, left_dim=1, right_dim=0):
    return lax.dot_general(
        left.astype(BF16),
        right.astype(BF16),
        (((left_dim,), (right_dim,)), ((), ())),
        preferred_element_type=F32,
    )


def halves(value):
    high = value.astype(BF16)
    return high, (value - high.astype(F32)).astype(BF16)


def mm_fine(left, right):
    left_high, left_low = halves(left)
    right_high, right_low = halves(right)
    return mm(left_high, right_high) + (mm(left_high, right_low) + mm(left_low, right_high))


def mm_ones(ones, value):
    high = value.astype(BF16)
    rest = value - high.astype(F32)
    middle = rest.astype(BF16)
    low = (rest - middle.astype(F32)).astype(BF16)
    return mm(ones, high) + (mm(ones, middle) + mm(ones, low))


def grids(length):
    rows = lax.broadcasted_iota(jnp.int32, (length, length), 0)
    cols = lax.broadcasted_iota(jnp.int32, (length, length), 1)
    return rows, cols


def lower_inverse(strict_part, rows, cols):
    length = strict_part.shape[0]
    unit = (rows == cols).astype(F32)
    base = 8
    nil = jnp.where(rows // base == cols // base, strict_part, 0.0)
    square = mm_fine(nil, nil)
    inverse = unit - nil
    inverse = inverse + mm_fine(inverse, square)
    inverse = inverse + mm_fine(inverse, mm_fine(square, square))
    size = base
    while size < length:
        joined = (rows // (2 * size) == cols // (2 * size)) & (rows // size != cols // size)
        corner = jnp.where(joined, strict_part, 0.0)
        inverse = inverse - mm_fine(inverse, mm_fine(corner, inverse))
        size *= 2
    return inverse


def shift_down(value, by):
    if by == 0:
        return value
    rows = lax.broadcasted_iota(jnp.int32, value.shape, 0)
    return jnp.where(rows >= by, pltpu.roll(value, by, 0), 0.0)


def shift_up(value, by):
    if by == 0:
        return value
    length = value.shape[0]
    rows = lax.broadcasted_iota(jnp.int32, value.shape, 0)
    return jnp.where(rows < length - by, pltpu.roll(value, length - by, 0), 0.0)


def conv_forward(value, taps):
    count = len(taps)
    total = taps[count - 1] * value
    for j in range(count - 1):
        total = total + taps[j] * shift_down(value, count - 1 - j)
    return total


def conv_backward(value, taps, grad):
    count = len(taps)
    grad_value = taps[count - 1] * grad
    grad_taps = []
    for j in range(count):
        by = count - 1 - j
        if by:
            grad_value = grad_value + taps[j] * shift_up(grad, by)
        grad_taps.append(jnp.sum(grad * shift_down(value, by), axis=0, keepdims=True))
    return grad_value, grad_taps


def silu_slope(value, gate):
    return gate * (1.0 + value * (1.0 - gate))


def pick_lane(block, lane):
    lanes = lax.broadcasted_iota(jnp.int32, block.shape, 1)
    return jnp.sum(jnp.where(lanes == lane, block, 0.0), axis=1, keepdims=True)


def softplus(value):
    return jnp.maximum(value, 0.0) + jnp.log1p(jnp.exp(-jnp.abs(value)))


def head_states(query_pre, key_pre, value_pre, alpha, beta, taps, rate, bias, masks):
    rows, cols, lower, strict = masks
    key_size = query_pre.shape[-1]
    query_conv = conv_forward(query_pre, taps[0])
    key_conv = conv_forward(key_pre, taps[1])
    value_conv = conv_forward(value_pre, taps[2])
    query_gate = jax.nn.sigmoid(query_conv)
    key_gate = jax.nn.sigmoid(key_conv)
    value_gate = jax.nn.sigmoid(value_conv)
    query_act = query_conv * query_gate
    key_act = key_conv * key_gate
    values = value_conv * value_gate
    query_scale = lax.rsqrt(jnp.sum(query_act * query_act, axis=-1, keepdims=True) + 1e-06)
    key_scale = lax.rsqrt(jnp.sum(key_act * key_act, axis=-1, keepdims=True) + 1e-06)
    query_unit = query_act * query_scale
    keys = key_act * key_scale
    queries = query_unit * key_size ** (-0.5)
    strength = jax.nn.sigmoid(beta)
    decay = -rate * softplus(alpha + bias)
    running = mm_ones(lower.astype(BF16), jnp.broadcast_to(decay, rows.shape))
    spread = running - running.T
    ratios = jnp.exp(jnp.where(lower, spread, 0.0)) * lower.astype(F32)
    key_key = mm(keys, keys, 1, 1)
    query_key = mm(queries, keys, 1, 1)
    key_ratio = jnp.where(strict, key_key * ratios, 0.0)
    weighting = query_key * ratios
    return dict(
        query_conv=query_conv,
        key_conv=key_conv,
        value_conv=value_conv,
        query_gate=query_gate,
        key_gate=key_gate,
        value_gate=value_gate,
        query_scale=query_scale,
        key_scale=key_scale,
        query_unit=query_unit,
        queries=queries,
        keys=keys,
        values=values,
        strength=strength,
        decay=decay,
        ratios=ratios,
        key_ratio=key_ratio,
        weighting=weighting,
    )


def read_taps(ref, lo, hi):
    return [ref[j : j + 1, lo:hi] for j in range(4)]


def mixer_forward_kernel(
    heads, length, query_ref, key_ref, value_ref, gate_ref, ab_ref, tq_ref, tk_ref, tv_ref, head_ref, gain_ref, mixed_ref, inverse_ref
):
    step = pl.program_id(0)
    per_step = inverse_ref.shape[0]
    sequences = query_ref.shape[0] // length
    key_size = query_ref.shape[1] // per_step
    value_size = value_ref.shape[1] // per_step
    rows, cols = grids(length)
    masks = (rows, cols, rows >= cols, rows > cols)
    gain = gain_ref[0:1, :]
    for local in range(per_step):
        head = step * per_step + local
        kc = slice(local * key_size, (local + 1) * key_size)
        vc = slice(local * value_size, (local + 1) * value_size)
        rate = jnp.exp(pick_lane(head_ref[0:1, :], head))
        bias = pick_lane(head_ref[1:2, :], head)
        taps = (
            read_taps(tq_ref, kc.start, kc.stop),
            read_taps(tk_ref, kc.start, kc.stop),
            read_taps(tv_ref, vc.start, vc.stop),
        )
        for seq in range(sequences):
            tr = slice(seq * length, (seq + 1) * length)
            ab = ab_ref[tr, :]
            alpha = pick_lane(ab, head)
            beta = pick_lane(ab, heads + head)
            s = head_states(
                query_ref[tr, kc], key_ref[tr, kc], value_ref[tr, vc], alpha, beta, taps, rate, bias, masks
            )
            inverse = lower_inverse(s["strength"] * s["key_ratio"], rows, cols)
            inverse_ref[local, seq] = inverse
            updates = mm(inverse, s["strength"] * s["values"])
            recur = mm(s["weighting"], updates)
            scale = lax.rsqrt(jnp.mean(recur * recur, axis=-1, keepdims=True) + 0.002)
            gate = gate_ref[tr, vc]
            mixed = recur * scale * gain * (gate * jax.nn.sigmoid(gate))
            mixed_ref[tr, vc] = mixed.astype(mixed_ref.dtype)


def mixer_backward_kernel(
    heads,
    length,
    query_ref,
    key_ref,
    value_ref,
    gate_ref,
    ab_ref,
    tq_ref,
    tk_ref,
    tv_ref,
    head_ref,
    gain_ref,
    inverse_ref,
    grad_ref,
    pre_a_ref,
    pre_b_ref,
    gtq_ref,
    gtk_ref,
    gtv_ref,
    ghead_ref,
    ggain_ref,
    gab_ref,
):
    step = pl.program_id(0)
    per_step = inverse_ref.shape[0]
    sequences = query_ref.shape[0] // length
    key_size = query_ref.shape[1] // per_step
    value_size = value_ref.shape[1] // per_step
    key_cols = heads * key_size
    value_cols = heads * value_size
    rows, cols = grids(length)
    lower, strict = rows >= cols, rows > cols
    masks = (rows, cols, lower, strict)
    upper = (rows <= cols).astype(BF16)
    gain = gain_ref[0:1, :]

    @pl.when(step == 0)
    def _():
        ghead_ref[...] = jnp.zeros_like(ghead_ref)
        ggain_ref[...] = jnp.zeros_like(ggain_ref)
        gab_ref[...] = jnp.zeros_like(gab_ref)

    lanes = lax.broadcasted_iota(jnp.int32, (length, LANES), 1)
    lane_row = lax.broadcasted_iota(jnp.int32, (1, LANES), 1)
    for local in range(per_step):
        head = step * per_step + local
        kc = slice(local * key_size, (local + 1) * key_size)
        vc = slice(local * value_size, (local + 1) * value_size)
        rate = jnp.exp(pick_lane(head_ref[0:1, :], head))
        bias = pick_lane(head_ref[1:2, :], head)
        taps = (
            read_taps(tq_ref, kc.start, kc.stop),
            read_taps(tk_ref, kc.start, kc.stop),
            read_taps(tv_ref, vc.start, vc.stop),
        )
        tap_totals = None
        gain_total = None
        rate_total = None
        bias_total = None
        for seq in range(sequences):
            tr = slice(seq * length, (seq + 1) * length)
            ab = ab_ref[tr, :]
            alpha = pick_lane(ab, head)
            beta = pick_lane(ab, heads + head)
            query_pre, key_pre, value_pre = query_ref[tr, kc], key_ref[tr, kc], value_ref[tr, vc]
            s = head_states(query_pre, key_pre, value_pre, alpha, beta, taps, rate, bias, masks)
            strength, keys, queries, values = s["strength"], s["keys"], s["queries"], s["values"]
            inverse = inverse_ref[local, seq]
            updates = mm(inverse, strength * values)
            recur = mm(s["weighting"], updates)
            scale = lax.rsqrt(jnp.mean(recur * recur, axis=-1, keepdims=True) + 0.002)
            normal = recur * scale
            gate = gate_ref[tr, vc]
            gate_sig = jax.nn.sigmoid(gate)
            gate_act = gate * gate_sig
            grad = grad_ref[tr, vc]
            grad_normal = grad * normal
            gain_part = jnp.sum(grad_normal * gate_act, axis=0, keepdims=True)
            grad_gate = grad_normal * gain * silu_slope(gate, gate_sig)
            grad_norm = grad * gain * gate_act
            grad_recur = scale * (grad_norm - normal * jnp.mean(grad_norm * normal, axis=-1, keepdims=True))
            grad_weight = jnp.where(lower, mm(grad_recur, updates, 1, 1), 0.0)
            grad_updates = mm(s["weighting"], grad_recur, 0, 0)
            grad_target = mm(inverse, grad_updates, 0, 0)
            grad_values = strength * grad_target
            grad_system = jnp.where(strict, -mm(grad_target, updates, 1, 1), 0.0)
            ratio_part = grad_system * s["key_ratio"]
            grad_strength = jnp.sum(grad_target * values, axis=-1, keepdims=True) + jnp.sum(
                ratio_part, axis=-1, keepdims=True
            )
            grad_kk = grad_system * strength * s["ratios"]
            grad_qk = grad_weight * s["ratios"]
            through = jnp.where(strict, ratio_part * strength + grad_weight * s["weighting"], 0.0)
            grad_running = jnp.sum(through - through.T, axis=-1, keepdims=True)
            grad_decay = mm_ones(upper, jnp.broadcast_to(grad_running, rows.shape))[:, 0:1]
            grad_keys = mm(grad_kk + grad_kk.T, keys) + mm(grad_qk, queries, 0, 0)
            grad_queries = mm(grad_qk, keys) * key_size ** (-0.5)
            query_unit = s["query_unit"]
            grad_query_act = s["query_scale"] * (
                grad_queries - query_unit * jnp.sum(grad_queries * query_unit, axis=-1, keepdims=True)
            )
            grad_key_act = s["key_scale"] * (
                grad_keys - keys * jnp.sum(grad_keys * keys, axis=-1, keepdims=True)
            )
            grad_query_pre, query_taps = conv_backward(
                query_pre, taps[0], grad_query_act * silu_slope(s["query_conv"], s["query_gate"])
            )
            grad_key_pre, key_taps = conv_backward(
                key_pre, taps[1], grad_key_act * silu_slope(s["key_conv"], s["key_gate"])
            )
            grad_value_pre, value_taps = conv_backward(
                value_pre, taps[2], grad_values * silu_slope(s["value_conv"], s["value_gate"])
            )
            grad_beta = grad_strength * strength * (1.0 - strength)
            grad_inner = -rate * grad_decay * jax.nn.sigmoid(alpha + bias)
            rate_part = jnp.sum(grad_decay * s["decay"], axis=0, keepdims=True)
            bias_part = jnp.sum(grad_inner, axis=0, keepdims=True)

            def put(ref, first, block):
                start = pl.multiple_of(first, LANES)
                ref[tr, pl.ds(start, block.shape[1])] = block.astype(ref.dtype)

            put(pre_a_ref, value_cols + head * key_size, grad_query_pre)
            put(pre_b_ref, value_cols + head * key_size, grad_key_pre)
            put(pre_a_ref, head * value_size, grad_value_pre)
            put(pre_b_ref, head * value_size, grad_gate)
            gab_ref[tr, :] = gab_ref[tr, :] + (
                jnp.where(lanes == head, grad_inner, 0.0) + jnp.where(lanes == heads + head, grad_beta, 0.0)
            )
            parts = (query_taps, key_taps, value_taps)
            if tap_totals is None:
                tap_totals, gain_total, rate_total, bias_total = parts, gain_part, rate_part, bias_part
            else:
                tap_totals = tuple(
                    [a + b for a, b in zip(one, two)] for one, two in zip(tap_totals, parts)
                )
                gain_total = gain_total + gain_part
                rate_total = rate_total + rate_part
                bias_total = bias_total + bias_part
        for j in range(4):
            gtq_ref[j : j + 1, kc] = tap_totals[0][j]
            gtk_ref[j : j + 1, kc] = tap_totals[1][j]
            gtv_ref[j : j + 1, vc] = tap_totals[2][j]
        ggain_ref[0:1, :] = ggain_ref[0:1, :] + gain_total
        ghead_ref[0:1, :] = ghead_ref[0:1, :] + jnp.where(lane_row == head, rate_total, 0.0)
        ghead_ref[1:2, :] = ghead_ref[1:2, :] + jnp.where(lane_row == head, bias_total, 0.0)

    @pl.when(step == heads // per_step - 1)
    def _():
        first = key_cols + value_cols
        pre_a_ref[:, first : first + LANES] = gab_ref[...].astype(pre_a_ref.dtype)


HEADS_PER_STEP = 2


def mixer_specs(tokens, heads, key_size, value_size):
    per_step = HEADS_PER_STEP
    wide_key, wide_value = per_step * key_size, per_step * value_size
    key_first = heads * value_size // wide_key
    ab_first = (heads * value_size + heads * key_size) // LANES
    return [
        pl.BlockSpec((tokens, wide_key), lambda h: (0, key_first + h)),
        pl.BlockSpec((tokens, wide_key), lambda h: (0, key_first + h)),
        pl.BlockSpec((tokens, wide_value), lambda h: (0, h)),
        pl.BlockSpec((tokens, wide_value), lambda h: (0, h)),
        pl.BlockSpec((tokens, LANES), lambda h: (0, ab_first)),
        pl.BlockSpec((8, wide_key), lambda h: (0, h)),
        pl.BlockSpec((8, wide_key), lambda h: (0, h)),
        pl.BlockSpec((8, wide_value), lambda h: (0, h)),
        pl.BlockSpec((8, LANES), lambda h: (0, 0)),
        pl.BlockSpec((8, value_size), lambda h: (0, 0)),
    ]


def mixer_forward(pre_a, pre_b, small, length, heads, key_size, value_size):
    tokens = pre_a.shape[0]
    per_step = HEADS_PER_STEP
    return pl.pallas_call(
        functools.partial(mixer_forward_kernel, heads, length),
        grid=(heads // per_step,),
        in_specs=mixer_specs(tokens, heads, key_size, value_size),
        out_specs=[
            pl.BlockSpec((tokens, per_step * value_size), lambda h: (0, h)),
            pl.BlockSpec((per_step, tokens // length, length, length), lambda h: (h, 0, 0, 0)),
        ],
        out_shape=[
            jax.ShapeDtypeStruct((tokens, heads * value_size), BF16),
            jax.ShapeDtypeStruct((heads, tokens // length, length, length), F32),
        ],
        compiler_params=pltpu.CompilerParams(vmem_limit_bytes=VMEM_LIMIT),
        name="mixer_forward",
    )(pre_a, pre_b, pre_a, pre_b, pre_a, *small)


def mixer_backward(pre_a, pre_b, small, inverse, grad, length, heads, key_size, value_size):
    tokens, width_a = pre_a.shape
    width_b = pre_b.shape[1]
    per_step = HEADS_PER_STEP
    wide_key, wide_value = per_step * key_size, per_step * value_size
    fixed = lambda h: (0, 0)
    moving = lambda h: (0, h)
    return pl.pallas_call(
        functools.partial(mixer_backward_kernel, heads, length),
        grid=(heads // per_step,),
        in_specs=mixer_specs(tokens, heads, key_size, value_size)
        + [
            pl.BlockSpec((per_step, tokens // length, length, length), lambda h: (h, 0, 0, 0)),
            pl.BlockSpec((tokens, wide_value), moving),
        ],
        out_specs=[
            pl.BlockSpec((tokens, width_a), fixed),
            pl.BlockSpec((tokens, width_b), fixed),
            pl.BlockSpec((8, wide_key), moving),
            pl.BlockSpec((8, wide_key), moving),
            pl.BlockSpec((8, wide_value), moving),
            pl.BlockSpec((8, LANES), fixed),
            pl.BlockSpec((8, value_size), fixed),
        ],
        out_shape=[
            jax.ShapeDtypeStruct((tokens, width_a), BF16),
            jax.ShapeDtypeStruct((tokens, width_b), BF16),
            jax.ShapeDtypeStruct((8, heads * key_size), F32),
            jax.ShapeDtypeStruct((8, heads * key_size), F32),
            jax.ShapeDtypeStruct((8, heads * value_size), F32),
            jax.ShapeDtypeStruct((8, LANES), F32),
            jax.ShapeDtypeStruct((8, value_size), F32),
        ],
        scratch_shapes=[pltpu.VMEM((tokens, LANES), F32)],
        compiler_params=pltpu.CompilerParams(vmem_limit_bytes=VMEM_LIMIT),
        name="mixer_backward",
    )(pre_a, pre_b, pre_a, pre_b, pre_a, *small, inverse, grad)


def swapped(value):
    return lax.ppermute(value, "section", [(0, 1), (1, 0)])


def pair_sum(value):
    return value + swapped(value)


SIDE = 4


class Ring:
    def __init__(self, axis):
        if axis == "y":
            self.name, self.position = "rep", lax.axis_index("rep")
            self.pairs = lambda by: [(y, (y + by) % SIDE) for y in range(SIDE)]
            return
        self.name = "fsdp"
        index = lax.axis_index("fsdp")
        z, x = index // SIDE, index % SIDE
        if axis == "x":
            self.position = x
            step = lambda z, x, by: z * SIDE + (x + by) % SIDE
        else:
            self.position = z
            step = lambda z, x, by: (z + by) % SIDE * SIDE + x
        self.pairs = lambda by: [
            (z * SIDE + x, step(z, x, by)) for z in range(SIDE) for x in range(SIDE)
        ]

    def move(self, value, by):
        return lax.ppermute(value, self.name, self.pairs(by))


def ring_gather(block, ring):
    count = block.shape[0] // 2
    from_left = ring.move(block, 1)
    from_right = ring.move(block, -1)
    far_first = ring.move(from_left[:count], 1)
    far_last = ring.move(from_right[count:], -1)
    return block, from_right, far_first, far_last, from_left


def torus_gather(shard, x_first):
    rows = shard.shape[0]
    if x_first:
        block = jnp.concatenate(ring_gather(shard, Ring("x")), axis=0)
        pieces = ring_gather(block, Ring("z"))
        return jnp.concatenate(pieces, axis=0), pieces[1]
    block = jnp.concatenate(ring_gather(shard, Ring("z")), axis=0)
    own, right, far_first, far_last, left = ring_gather(block, Ring("x"))
    cut = lambda piece, k: piece[k * rows : (k + 1) * rows]
    rows_of = []
    for kz in range(SIDE):
        far = cut(far_first, kz) if kz < SIDE // 2 else cut(far_last, kz - SIDE // 2)
        rows_of += [cut(own, kz), cut(right, kz), far, cut(left, kz)]
    return jnp.concatenate(rows_of, axis=0), right


def added(first, *others):
    total = first.astype(F32)
    for other in others:
        total = total + other.astype(F32)
    return total.astype(BF16)


def ring_scatter(parts, ring):
    ahead, behind, rest, own = parts
    count = own.shape[0] // 2
    from_left = ring.move(ahead, 1)
    from_right = ring.move(behind, -1)
    next_left = ring.move(added(rest[:count], from_left[:count]), 1)
    next_right = ring.move(added(rest[count:], from_right[:count]), -1)
    return jnp.concatenate(
        [
            added(own[:count], next_left, from_right[count:]),
            added(own[count:], from_left[count:], next_right),
        ],
        axis=0,
    )


def torus_scatter(chunks, x_first):
    first, second = ("x", "z") if x_first else ("z", "x")

    def parts(total, make):
        quarter, half = total // SIDE, total // SIDE // 2
        join = lambda one, two: make([(one, one + half), (two, two + half)])
        return [
            join(2 * quarter, quarter + half),
            join(2 * quarter + half, 3 * quarter),
            join(quarter, 3 * quarter + half),
            make([(0, quarter)]),
        ]

    block = ring_scatter(parts(chunks.total, chunks.make), Ring(first))
    make = lambda cuts: jnp.concatenate([block[i:j] for i, j in cuts], axis=0)
    return ring_scatter(parts(block.shape[0], make), Ring(second))


class Chunks:
    def __init__(self, products):
        self.products = products
        self.total = products[0][0].shape[1]

    def make(self, cuts):
        blocks = []
        for left, right, extra in self.products:
            rows = jnp.concatenate([left[:, i:j] for i, j in cuts], axis=1)
            block = dot_tn(rows, right)
            if extra is not None:
                block = block + jnp.concatenate([extra[i:j] for i, j in cuts], axis=0)
            blocks.append(block.astype(BF16))
        return jnp.concatenate(blocks, axis=1)


def own_order(rows):
    index = lax.axis_index("fsdp")
    z, x = index // SIDE, index % SIDE
    place = jnp.arange(SIDE * SIDE * rows, dtype=jnp.int32)
    by_z, by_x, offset = place // (SIDE * rows), place // rows % SIDE, place % rows
    source = ((z + by_z) % SIDE * SIDE + (x + by_x) % SIDE) * rows + offset
    return (place[:, None] == source[None, :]).astype(BF16)


def flipped_order(rows):
    place = jnp.arange(SIDE * SIDE * rows, dtype=jnp.int32)
    by_x, by_z, offset = place // (SIDE * rows), place // rows % SIDE, place % rows
    source = (by_z * SIDE + by_x) * rows + offset
    return (place[:, None] == source[None, :]).astype(BF16)


def rep_sum(value):
    near = [(0, 1), (1, 0), (2, 3), (3, 2)]
    across = [(0, 3), (3, 0), (1, 2), (2, 1)]
    count = value.shape[0] // 2
    done = []
    for part, order in ((value[:count], (near, across)), (value[count:], (across, near))):
        for pairs in order:
            part = added(part, lax.ppermute(part, "rep", pairs))
        done.append(part)
    return jnp.concatenate(done, axis=0)


def dot(left, right):
    return jnp.dot(left, right, preferred_element_type=F32)


def dot_nt(left, right):
    return lax.dot_general(left, right, (((1,), (1,)), ((), ())), preferred_element_type=F32)


def dot_tn(left, right):
    return lax.dot_general(left, right, (((0,), (0,)), ((), ())), preferred_element_type=F32)


def inverse_rms(value):
    return lax.rsqrt(jnp.mean(value * value, axis=-1, keepdims=True) + 1e-06)


def norm_backward(value, gain, grad):
    scale = inverse_rms(value)
    unit = value * scale
    inner = grad * gain
    grad_value = scale * (inner - unit * jnp.mean(inner * unit, axis=-1, keepdims=True))
    return grad_value, jnp.sum(grad * unit, axis=0)


def per_device(
    inputs,
    out_grad,
    mixer_norm_gain,
    w_query,
    w_key,
    w_value,
    w_gate,
    w_alpha,
    w_beta,
    log_rate,
    dt_bias,
    conv_query,
    conv_key,
    conv_value,
    out_gain,
    w_out,
    gain_ffn,
    w_ffgate,
    w_ffup,
    w_ffdown,
):
    core = lax.axis_index("section")
    first_core = core == 0
    micro, _, length, width = inputs.shape
    tokens = micro * length
    members = lax.axis_size("fsdp")
    cores = 2
    all_heads = log_rate.shape[1]
    heads = all_heads // cores
    key_size = w_query.shape[2] // all_heads
    value_size = w_value.shape[2] // all_heads
    key_cols, value_cols = heads * key_size, heads * value_size
    ffn_cols = w_ffgate.shape[2] // cores
    rows = w_query.shape[1]
    taps = conv_query.shape[1]
    out_rows, down_rows = w_out.shape[1], w_ffdown.shape[1]
    value_split = conv_value.shape[2] // rows
    gain_rows = out_gain.shape[1]

    def choose(first, second):
        return jnp.where(first_core, first, second)

    small_cols = jnp.concatenate(
        [
            mixer_norm_gain[0][:, None],
            gain_ffn[0][:, None],
            conv_query[0].T,
            conv_key[0].T,
            conv_value[0].reshape(taps * value_split, rows).T,
            jnp.pad(out_gain[0], (0, rows - gain_rows))[:, None],
        ],
        axis=1,
    )
    small_count = small_cols.shape[1]
    ab_cols = 2 * heads
    spare = PAD - ab_cols - small_count
    main_a = value_cols + key_cols
    split = 2 * LANES
    out_first, down_first = ffn_cols, ffn_cols + value_cols

    lane_rows = out_rows + down_rows
    both_t = jnp.concatenate([w_out[0].T, w_ffdown[0].T], axis=1)
    both_t = jnp.pad(both_t, ((0, 0), (0, -lane_rows % LANES))).reshape(members, rows, -1)
    both_t = lax.all_to_all(both_t, "fsdp", split_axis=0, concat_axis=0, tiled=True)
    out_t = both_t[:, :, :out_rows].transpose(1, 0, 2).reshape(rows, members * out_rows)
    down_t = both_t[:, :, out_rows:lane_rows].transpose(1, 0, 2).reshape(rows, members * down_rows)

    def cut(w, k):
        n = w.shape[1] // cores
        return w[:, k * n : (k + 1) * n]

    def in_piece(k):
        return jnp.concatenate(
            [cut(w[0], k) for w in (w_value, w_query, w_alpha, w_beta)]
            + [small_cols, jnp.zeros((rows, spare), BF16)]
            + [cut(w[0], k) for w in (w_gate, w_key)],
            axis=1,
        )

    def ffn_piece(k):
        down = cut(down_t, k)
        return jnp.concatenate(
            [cut(w_ffgate[0], k), cut(out_t, k), down[:, :split], cut(w_ffup[0], k), down[:, split:]], axis=1
        )

    def both(make):
        left, right = make(0), make(1)
        own, sent = choose(left, right), choose(right, left)
        received = swapped(sent)
        return choose(own, received), choose(received, own)

    in_pieces = both(in_piece)
    ffn_pieces = both(ffn_piece)
    in_a = main_a + PAD
    ffn_a = down_first + split
    rate_rows = jnp.stack([log_rate[0], dt_bias[0]])
    other_rates = swapped(rate_rows)
    rates = (choose(rate_rows, other_rates), choose(other_rates, rate_rows))
    order = own_order(rows)
    flip = flipped_order(rows)

    def ordered(value):
        return dot(value, order)

    def unordered(value):
        high = value.astype(BF16)
        rest = value - high.astype(F32)
        middle = rest.astype(BF16)
        low = (rest - middle.astype(F32)).astype(BF16)
        return dot_nt(high, order) + (dot_nt(middle, order) + dot_nt(low, order))

    def flipped(value):
        return dot(value, flip).astype(BF16)

    def after(value, token):
        return value if token is None else lax.optimization_barrier((value, token))[0]

    def fetch(pieces, wide, token):
        pieces = after(pieces, token)
        full_a, token_a = torus_gather(pieces[:, :wide], True)
        full_b, token_b = torus_gather(pieces[:, wide:], False)
        return full_a, full_b, (token_a, token_b)

    def small_params(in_full, layer):
        first = main_a + ab_cols
        small_own = in_full[:, first : first + small_count].T
        small = small_own.astype(F32) if layer else dot_nt(small_own, order)
        at = 2
        conv_q = small[at : at + taps]
        conv_k = small[at + taps : at + 2 * taps]
        at += 2 * taps
        conv_v = small[at : at + taps * value_split].reshape(taps, value_split, members, rows)
        conv_v = conv_v.transpose(0, 2, 1, 3).reshape(taps, members * value_split * rows)
        at += taps * value_split
        gain_out = small[at].reshape(members, rows)[:, :gain_rows].reshape(1, members * gain_rows)

        def own_cols(value, count):
            mine = choose(value[:, :count], value[:, count:])
            return jnp.pad(mine, ((0, 8 - value.shape[0]), (0, 0)))

        rate = own_cols(rates[layer], heads)
        smalls = (
            own_cols(conv_q, key_cols),
            own_cols(conv_k, key_cols),
            own_cols(conv_v, value_cols),
            jnp.pad(rate, ((0, 0), (0, LANES - heads))),
            jnp.pad(gain_out, ((0, 7), (0, 0))),
        )
        return small_own[0].astype(F32), small_own[1].astype(F32), smalls

    def forward_layer(source, in_full, ffn_full, params):
        in_w, in_v = in_full
        ffn_w, ffn_v = ffn_full
        gain_mix, gain_in, smalls = params
        normed = (source * inverse_rms(source) * gain_mix).astype(BF16)
        pre_a, pre_b = dot(normed, in_w), dot(normed, in_v)
        mixed, inverse = mixer_forward(pre_a, pre_b, smalls, length, heads, key_size, value_size)
        after_mix = source + pair_sum(dot_nt(mixed, ffn_w[:, out_first:down_first]))
        normed_ffn = (after_mix * inverse_rms(after_mix) * gain_in).astype(BF16)
        gate_act = dot(normed_ffn, ffn_w[:, :ffn_cols])
        up_act = dot(normed_ffn, ffn_v[:, :ffn_cols])
        hidden = (gate_act * jax.nn.sigmoid(gate_act) * up_act).astype(BF16)
        part = dot_nt(hidden[:, :split], ffn_w[:, down_first:]) + dot_nt(hidden[:, split:], ffn_v[:, ffn_cols:])
        layer_out = after_mix + pair_sum(part)
        return layer_out, (source, normed, pre_a, pre_b, inverse, mixed, after_mix, normed_ffn, gate_act, up_act, hidden)

    def scattered(blocks):
        full = jnp.concatenate([block.astype(BF16) for block in blocks], axis=1)
        return lax.psum_scatter(full, "fsdp", scatter_dimension=0, tiled=True)

    def backward_layer(grad_top, saved, in_full, ffn_full, params, by_ring):
        source, normed, pre_a, pre_b, inverse, mixed, after_mix, normed_ffn, gate_act, up_act, hidden = saved
        in_w, in_v = in_full
        ffn_w, ffn_v = ffn_full
        gain_mix, gain_in, smalls = params
        down_grad = grad_top.astype(BF16)
        hidden_grad = jnp.concatenate(
            [dot(down_grad, ffn_w[:, down_first:]), dot(down_grad, ffn_v[:, ffn_cols:])], axis=1
        )
        gate_sig = jax.nn.sigmoid(gate_act)
        gate_grad = (hidden_grad * up_act * silu_slope(gate_act, gate_sig)).astype(BF16)
        up_grad = (hidden_grad * (gate_act * gate_sig)).astype(BF16)
        ffn_in_grad = pair_sum(dot_nt(gate_grad, ffn_w[:, :ffn_cols]) + dot_nt(up_grad, ffn_v[:, :ffn_cols]))
        residual, grad_gain_ffn = norm_backward(after_mix, gain_in, ffn_in_grad)
        mix_grad = grad_top + residual
        mix_low = mix_grad.astype(BF16)
        mixed_grad = dot(mix_low, ffn_w[:, out_first:down_first])
        if by_ring:
            grad_ffn = (
                torus_scatter(
                    Chunks(
                        [
                            (flipped(normed_ffn), gate_grad, None),
                            (flipped(mix_low), mixed, None),
                            (flipped(down_grad), hidden[:, :split], None),
                        ]
                    ),
                    True,
                ),
                torus_scatter(Chunks([(normed_ffn, up_grad, None), (down_grad, hidden[:, split:], None)]), False),
            )
            grad_ffn = jnp.concatenate(grad_ffn, axis=1)
        else:
            grad_ffn = scattered(
                [
                    dot_tn(normed_ffn, gate_grad),
                    dot_tn(mix_low, mixed),
                    dot_tn(down_grad, hidden[:, :split]),
                    dot_tn(normed_ffn, up_grad),
                    dot_tn(down_grad, hidden[:, split:]),
                ]
            )
        grad_ffn = rep_sum(grad_ffn)
        pre_a_grad, pre_b_grad, gtq, gtk, gtv, ghead, ggain = mixer_backward(
            pre_a, pre_b, smalls, inverse, mixed_grad, length, heads, key_size, value_size
        )
        normed_grad = pair_sum(dot_nt(pre_a_grad, in_w) + dot_nt(pre_b_grad, in_v))
        source_part, grad_gain_mix = norm_backward(source, gain_mix, normed_grad)
        source_grad = mix_grad + source_part

        def whole_cols(value):
            zeros = jnp.zeros_like(value)
            return choose(
                jnp.concatenate([value, zeros], axis=1), jnp.concatenate([zeros, value], axis=1)
            )

        conv_v = whole_cols(gtv[:taps]).reshape(taps, members, value_split, rows)
        conv_v = conv_v.transpose(0, 2, 1, 3).reshape(taps * value_split, members * rows)
        gain_out = ggain[0].reshape(members, gain_rows)
        head_part = whole_cols(ghead[:2, :heads]).reshape(1, 2 * all_heads)
        head_part = jnp.broadcast_to(head_part, (members, 2 * all_heads))
        tail = jnp.concatenate(
            [gain_out, head_part, jnp.zeros((members, rows - gain_rows - 2 * all_heads), F32)], axis=1
        )
        once = first_core.astype(F32)
        gains = jnp.stack([grad_gain_mix, grad_gain_ffn]) * once
        others = jnp.concatenate(
            [whole_cols(gtq[:taps]), whole_cols(gtk[:taps]), conv_v, tail.reshape(1, members * rows)], axis=0
        )
        others = others.astype(BF16)
        others = ordered(others).astype(BF16) if by_ring else others
        small = jnp.concatenate([gains.astype(BF16), others], axis=0)
        small = jnp.concatenate(
            [jnp.zeros((ab_cols, width), BF16), small, jnp.zeros((spare, width), BF16)], axis=0
        )
        if by_ring:
            small = lax.dot_general(flip, small, (((0,), (1,)), ((), ())), preferred_element_type=F32)
            turned = flipped(normed)
            grad_in = (
                torus_scatter(
                    Chunks([(turned, pre_a_grad[:, :main_a], None), (turned, pre_a_grad[:, main_a:], small)]), True
                ),
                torus_scatter(Chunks([(normed, pre_b_grad, None)]), False),
            )
            grad_in = jnp.concatenate(grad_in, axis=1)
        else:
            grad_in = scattered(
                [
                    dot_tn(normed, pre_a_grad[:, :main_a]),
                    dot_tn(normed, pre_a_grad[:, main_a:]) + small.T.astype(F32),
                    dot_tn(normed, pre_b_grad),
                ]
            )
        grad_in = rep_sum(grad_in)
        return source_grad, grad_in, grad_ffn

    def to_owner(first, second):
        own = choose(first, second)
        received = swapped(choose(second, first))
        return choose(own, received), choose(received, own)

    source = ordered(inputs.reshape(tokens, width))
    in_0a, in_0b, token = fetch(in_pieces[0], in_a, None)
    ffn_0a, ffn_0b, token = fetch(ffn_pieces[0], ffn_a, token)
    in_1 = lax.all_gather(in_pieces[1], "fsdp", axis=0, tiled=True)
    ffn_1 = lax.all_gather(ffn_pieces[1], "fsdp", axis=0, tiled=True)
    in_0, ffn_0 = (in_0a, in_0b), (ffn_0a, ffn_0b)
    in_1, ffn_1 = (in_1[:, :in_a], in_1[:, in_a:]), (ffn_1[:, :ffn_a], ffn_1[:, ffn_a:])
    params_0, params_1 = small_params(in_0a, 0), small_params(in_1[0], 1)
    first_out, first_saved = forward_layer(source, in_0, ffn_0, params_0)
    middle = dot_nt(first_out.astype(BF16), order)
    block_out, second_saved = forward_layer(middle, in_1, ffn_1, params_1)
    cotangent = out_grad.reshape(tokens, width).astype(F32)
    second_grad, second_in, second_ffn = backward_layer(cotangent, second_saved, in_1, ffn_1, params_1, False)
    input_grad, first_in, first_ffn = backward_layer(
        ordered(second_grad.astype(BF16)), first_saved, in_0, ffn_0, params_0, True
    )
    in_left, in_right = to_owner(first_in, second_in)
    ffn_left, ffn_right = to_owner(first_ffn, second_ffn)

    def joined(left, right, first, count):
        span = slice(first, first + count)
        return jnp.concatenate([left[:, span], right[:, span]], axis=1).astype(F32)[None]

    gate_first = main_a + PAD
    up_first = down_first + split
    down_rest = up_first + ffn_cols
    full_out = jnp.concatenate(
        [side[:, out_first:down_first] for side in (ffn_left, ffn_right)], axis=1
    ).reshape(rows, members, out_rows)
    full_down = jnp.concatenate(
        [part for side in (ffn_left, ffn_right) for part in (side[:, down_first:up_first], side[:, down_rest:])], axis=1
    ).reshape(rows, members, down_rows)
    back = jnp.concatenate([full_out, full_down], axis=2).transpose(1, 0, 2)
    back = jnp.pad(back, ((0, 0), (0, 0), (0, -lane_rows % LANES)))
    back = lax.all_to_all(back, "fsdp", split_axis=0, concat_axis=0, tiled=True).reshape(width, -1)
    grad_out = back[:, :out_rows].T.astype(F32)
    grad_down = back[:, out_rows:lane_rows].T.astype(F32)

    first = main_a + ab_cols
    small = in_left[:, first : first + small_count].astype(F32) + in_right[:, first : first + small_count].astype(F32)
    small = small.T
    tail = small[small_count - 1]
    conv_at = 2 + 2 * taps
    head_grads = tail[gain_rows : gain_rows + 2 * all_heads].reshape(2, all_heads)
    edges = choose(unordered(input_grad), block_out).reshape(1, micro, 1, length, width)
    return (
        edges,
        small[0][None],
        joined(in_left, in_right, value_cols, key_cols),
        joined(in_left, in_right, gate_first + value_cols, key_cols),
        joined(in_left, in_right, 0, value_cols),
        joined(in_left, in_right, gate_first, value_cols),
        joined(in_left, in_right, main_a, heads),
        joined(in_left, in_right, main_a + heads, heads),
        head_grads[0:1],
        head_grads[1:2],
        small[2 : 2 + taps][None],
        small[2 + taps : 2 + 2 * taps][None],
        small[conv_at : conv_at + taps * value_split].reshape(1, taps, value_split * rows),
        tail[:gain_rows][None],
        grad_out[None],
        small[1][None],
        joined(ffn_left, ffn_right, 0, ffn_cols),
        joined(ffn_left, ffn_right, up_first, ffn_cols),
        grad_down[None],
    )


def solution(mesh):
    across = P("section", "fsdp", None)
    lanes = P("section", None, "fsdp")
    vector = P("section", "fsdp")
    rates = P("section", None)
    tokens = P(None, ("rep", "fsdp"), None, None)
    placed = (
        (tokens, tokens, vector)
        + (across,) * 6
        + (rates, rates, lanes, lanes, lanes, vector, across, vector, across, across, across)
    )
    return jax.shard_map(
        per_device,
        mesh=mesh,
        in_specs=placed,
        out_specs=(P("section", None, ("rep", "fsdp"), None, None), vector)
        + (across,) * 6
        + (rates, rates, lanes, lanes, lanes, vector, across, vector, across, across, across),
        check_vma=False,
    )
```

```python
import functools

import jax
import jax.numpy as jnp
from jax import lax
from jax.experimental import pallas as pl
from jax.experimental.pallas import tpu as pltpu
from jax.sharding import PartitionSpec as P

F32 = jnp.float32
BF16 = jnp.bfloat16
PAD = 128
LANES = 128
VMEM_LIMIT = 56 * 1024 * 1024


def mm(left, right, left_dim=1, right_dim=0):
    return lax.dot_general(
        left.astype(BF16),
        right.astype(BF16),
        (((left_dim,), (right_dim,)), ((), ())),
        preferred_element_type=F32,
    )


def halves(value):
    high = value.astype(BF16)
    return high, (value - high.astype(F32)).astype(BF16)


def mm_fine(left, right):
    left_high, left_low = halves(left)
    right_high, right_low = halves(right)
    return mm(left_high, right_high) + (mm(left_high, right_low) + mm(left_low, right_high))


def mm_ones(ones, value):
    high = value.astype(BF16)
    rest = value - high.astype(F32)
    middle = rest.astype(BF16)
    low = (rest - middle.astype(F32)).astype(BF16)
    return mm(ones, high) + (mm(ones, middle) + mm(ones, low))


def grids(length):
    rows = lax.broadcasted_iota(jnp.int32, (length, length), 0)
    cols = lax.broadcasted_iota(jnp.int32, (length, length), 1)
    return rows, cols


def lower_inverse(strict_part, rows, cols):
    length = strict_part.shape[0]
    unit = (rows == cols).astype(F32)
    base = 8
    nil = jnp.where(rows // base == cols // base, strict_part, 0.0)
    square = mm_fine(nil, nil)
    inverse = unit - nil
    inverse = inverse + mm_fine(inverse, square)
    inverse = inverse + mm_fine(inverse, mm_fine(square, square))
    size = base
    while size < length:
        joined = (rows // (2 * size) == cols // (2 * size)) & (rows // size != cols // size)
        corner = jnp.where(joined, strict_part, 0.0)
        inverse = inverse - mm_fine(inverse, mm_fine(corner, inverse))
        size *= 2
    return inverse


def shift_down(value, by):
    if by == 0:
        return value
    rows = lax.broadcasted_iota(jnp.int32, value.shape, 0)
    return jnp.where(rows >= by, pltpu.roll(value, by, 0), 0.0)


def shift_up(value, by):
    if by == 0:
        return value
    length = value.shape[0]
    rows = lax.broadcasted_iota(jnp.int32, value.shape, 0)
    return jnp.where(rows < length - by, pltpu.roll(value, length - by, 0), 0.0)


def conv_forward(value, taps):
    count = len(taps)
    total = taps[count - 1] * value
    for j in range(count - 1):
        total = total + taps[j] * shift_down(value, count - 1 - j)
    return total


def conv_backward(value, taps, grad):
    count = len(taps)
    grad_value = taps[count - 1] * grad
    grad_taps = []
    for j in range(count):
        by = count - 1 - j
        if by:
            grad_value = grad_value + taps[j] * shift_up(grad, by)
        grad_taps.append(jnp.sum(grad * shift_down(value, by), axis=0, keepdims=True))
    return grad_value, grad_taps


def silu_slope(value, gate):
    return gate * (1.0 + value * (1.0 - gate))


def pick_lane(block, lane):
    lanes = lax.broadcasted_iota(jnp.int32, block.shape, 1)
    return jnp.sum(jnp.where(lanes == lane, block, 0.0), axis=1, keepdims=True)


def softplus(value):
    return jnp.maximum(value, 0.0) + jnp.log1p(jnp.exp(-jnp.abs(value)))


def head_states(query_pre, key_pre, value_pre, alpha, beta, taps, rate, bias, masks):
    rows, cols, lower, strict = masks
    key_size = query_pre.shape[-1]
    query_conv = conv_forward(query_pre, taps[0])
    key_conv = conv_forward(key_pre, taps[1])
    value_conv = conv_forward(value_pre, taps[2])
    query_gate = jax.nn.sigmoid(query_conv)
    key_gate = jax.nn.sigmoid(key_conv)
    value_gate = jax.nn.sigmoid(value_conv)
    query_act = query_conv * query_gate
    key_act = key_conv * key_gate
    values = value_conv * value_gate
    query_scale = lax.rsqrt(jnp.sum(query_act * query_act, axis=-1, keepdims=True) + 1e-06)
    key_scale = lax.rsqrt(jnp.sum(key_act * key_act, axis=-1, keepdims=True) + 1e-06)
    query_unit = query_act * query_scale
    keys = key_act * key_scale
    queries = query_unit * key_size ** (-0.5)
    strength = jax.nn.sigmoid(beta)
    decay = -rate * softplus(alpha + bias)
    running = mm_ones(lower.astype(BF16), jnp.broadcast_to(decay, rows.shape))
    spread = running - running.T
    ratios = jnp.exp(jnp.where(lower, spread, 0.0)) * lower.astype(F32)
    key_key = mm(keys, keys, 1, 1)
    query_key = mm(queries, keys, 1, 1)
    key_ratio = jnp.where(strict, key_key * ratios, 0.0)
    weighting = query_key * ratios
    return dict(
        query_conv=query_conv,
        key_conv=key_conv,
        value_conv=value_conv,
        query_gate=query_gate,
        key_gate=key_gate,
        value_gate=value_gate,
        query_scale=query_scale,
        key_scale=key_scale,
        query_unit=query_unit,
        queries=queries,
        keys=keys,
        values=values,
        strength=strength,
        decay=decay,
        ratios=ratios,
        key_ratio=key_ratio,
        weighting=weighting,
    )


def read_taps(ref, lo, hi):
    return [ref[j : j + 1, lo:hi] for j in range(4)]


def mixer_forward_kernel(
    heads, length, query_ref, key_ref, value_ref, gate_ref, ab_ref, tq_ref, tk_ref, tv_ref, head_ref, gain_ref, mixed_ref, inverse_ref
):
    step = pl.program_id(0)
    per_step = inverse_ref.shape[0]
    sequences = query_ref.shape[0] // length
    key_size = query_ref.shape[1] // per_step
    value_size = value_ref.shape[1] // per_step
    rows, cols = grids(length)
    masks = (rows, cols, rows >= cols, rows > cols)
    gain = gain_ref[0:1, :]
    for local in range(per_step):
        head = step * per_step + local
        kc = slice(local * key_size, (local + 1) * key_size)
        vc = slice(local * value_size, (local + 1) * value_size)
        rate = jnp.exp(pick_lane(head_ref[0:1, :], head))
        bias = pick_lane(head_ref[1:2, :], head)
        taps = (
            read_taps(tq_ref, kc.start, kc.stop),
            read_taps(tk_ref, kc.start, kc.stop),
            read_taps(tv_ref, vc.start, vc.stop),
        )
        for seq in range(sequences):
            tr = slice(seq * length, (seq + 1) * length)
            ab = ab_ref[tr, :]
            alpha = pick_lane(ab, head)
            beta = pick_lane(ab, heads + head)
            s = head_states(
                query_ref[tr, kc], key_ref[tr, kc], value_ref[tr, vc], alpha, beta, taps, rate, bias, masks
            )
            inverse = lower_inverse(s["strength"] * s["key_ratio"], rows, cols)
            inverse_ref[local, seq] = inverse
            updates = mm(inverse, s["strength"] * s["values"])
            recur = mm(s["weighting"], updates)
            scale = lax.rsqrt(jnp.mean(recur * recur, axis=-1, keepdims=True) + 0.002)
            gate = gate_ref[tr, vc]
            mixed = recur * scale * gain * (gate * jax.nn.sigmoid(gate))
            mixed_ref[tr, vc] = mixed.astype(mixed_ref.dtype)


def mixer_backward_kernel(
    heads,
    length,
    query_ref,
    key_ref,
    value_ref,
    gate_ref,
    ab_ref,
    tq_ref,
    tk_ref,
    tv_ref,
    head_ref,
    gain_ref,
    inverse_ref,
    grad_ref,
    pre_a_ref,
    pre_b_ref,
    gtq_ref,
    gtk_ref,
    gtv_ref,
    ghead_ref,
    ggain_ref,
    gab_ref,
):
    step = pl.program_id(0)
    per_step = inverse_ref.shape[0]
    sequences = query_ref.shape[0] // length
    key_size = query_ref.shape[1] // per_step
    value_size = value_ref.shape[1] // per_step
    key_cols = heads * key_size
    value_cols = heads * value_size
    rows, cols = grids(length)
    lower, strict = rows >= cols, rows > cols
    masks = (rows, cols, lower, strict)
    upper = (rows <= cols).astype(BF16)
    gain = gain_ref[0:1, :]

    @pl.when(step == 0)
    def _():
        ghead_ref[...] = jnp.zeros_like(ghead_ref)
        ggain_ref[...] = jnp.zeros_like(ggain_ref)
        gab_ref[...] = jnp.zeros_like(gab_ref)

    lanes = lax.broadcasted_iota(jnp.int32, (length, LANES), 1)
    lane_row = lax.broadcasted_iota(jnp.int32, (1, LANES), 1)
    for local in range(per_step):
        head = step * per_step + local
        kc = slice(local * key_size, (local + 1) * key_size)
        vc = slice(local * value_size, (local + 1) * value_size)
        rate = jnp.exp(pick_lane(head_ref[0:1, :], head))
        bias = pick_lane(head_ref[1:2, :], head)
        taps = (
            read_taps(tq_ref, kc.start, kc.stop),
            read_taps(tk_ref, kc.start, kc.stop),
            read_taps(tv_ref, vc.start, vc.stop),
        )
        tap_totals = None
        gain_total = None
        rate_total = None
        bias_total = None
        for seq in range(sequences):
            tr = slice(seq * length, (seq + 1) * length)
            ab = ab_ref[tr, :]
            alpha = pick_lane(ab, head)
            beta = pick_lane(ab, heads + head)
            query_pre, key_pre, value_pre = query_ref[tr, kc], key_ref[tr, kc], value_ref[tr, vc]
            s = head_states(query_pre, key_pre, value_pre, alpha, beta, taps, rate, bias, masks)
            strength, keys, queries, values = s["strength"], s["keys"], s["queries"], s["values"]
            inverse = inverse_ref[local, seq]
            updates = mm(inverse, strength * values)
            recur = mm(s["weighting"], updates)
            scale = lax.rsqrt(jnp.mean(recur * recur, axis=-1, keepdims=True) + 0.002)
            normal = recur * scale
            gate = gate_ref[tr, vc]
            gate_sig = jax.nn.sigmoid(gate)
            gate_act = gate * gate_sig
            grad = grad_ref[tr, vc]
            grad_normal = grad * normal
            gain_part = jnp.sum(grad_normal * gate_act, axis=0, keepdims=True)
            grad_gate = grad_normal * gain * silu_slope(gate, gate_sig)
            grad_norm = grad * gain * gate_act
            grad_recur = scale * (grad_norm - normal * jnp.mean(grad_norm * normal, axis=-1, keepdims=True))
            grad_weight = jnp.where(lower, mm(grad_recur, updates, 1, 1), 0.0)
            grad_updates = mm(s["weighting"], grad_recur, 0, 0)
            grad_target = mm(inverse, grad_updates, 0, 0)
            grad_values = strength * grad_target
            grad_system = jnp.where(strict, -mm(grad_target, updates, 1, 1), 0.0)
            ratio_part = grad_system * s["key_ratio"]
            grad_strength = jnp.sum(grad_target * values, axis=-1, keepdims=True) + jnp.sum(
                ratio_part, axis=-1, keepdims=True
            )
            grad_kk = grad_system * strength * s["ratios"]
            grad_qk = grad_weight * s["ratios"]
            through = jnp.where(strict, ratio_part * strength + grad_weight * s["weighting"], 0.0)
            grad_running = jnp.sum(through - through.T, axis=-1, keepdims=True)
            grad_decay = mm_ones(upper, jnp.broadcast_to(grad_running, rows.shape))[:, 0:1]
            grad_keys = mm(grad_kk + grad_kk.T, keys) + mm(grad_qk, queries, 0, 0)
            grad_queries = mm(grad_qk, keys) * key_size ** (-0.5)
            query_unit = s["query_unit"]
            grad_query_act = s["query_scale"] * (
                grad_queries - query_unit * jnp.sum(grad_queries * query_unit, axis=-1, keepdims=True)
            )
            grad_key_act = s["key_scale"] * (
                grad_keys - keys * jnp.sum(grad_keys * keys, axis=-1, keepdims=True)
            )
            grad_query_pre, query_taps = conv_backward(
                query_pre, taps[0], grad_query_act * silu_slope(s["query_conv"], s["query_gate"])
            )
            grad_key_pre, key_taps = conv_backward(
                key_pre, taps[1], grad_key_act * silu_slope(s["key_conv"], s["key_gate"])
            )
            grad_value_pre, value_taps = conv_backward(
                value_pre, taps[2], grad_values * silu_slope(s["value_conv"], s["value_gate"])
            )
            grad_beta = grad_strength * strength * (1.0 - strength)
            grad_inner = -rate * grad_decay * jax.nn.sigmoid(alpha + bias)
            rate_part = jnp.sum(grad_decay * s["decay"], axis=0, keepdims=True)
            bias_part = jnp.sum(grad_inner, axis=0, keepdims=True)

            def put(ref, first, block):
                start = pl.multiple_of(first, LANES)
                ref[tr, pl.ds(start, block.shape[1])] = block.astype(ref.dtype)

            put(pre_a_ref, value_cols + head * key_size, grad_query_pre)
            put(pre_b_ref, value_cols + head * key_size, grad_key_pre)
            put(pre_a_ref, head * value_size, grad_value_pre)
            put(pre_b_ref, head * value_size, grad_gate)
            gab_ref[tr, :] = gab_ref[tr, :] + (
                jnp.where(lanes == head, grad_inner, 0.0) + jnp.where(lanes == heads + head, grad_beta, 0.0)
            )
            parts = (query_taps, key_taps, value_taps)
            if tap_totals is None:
                tap_totals, gain_total, rate_total, bias_total = parts, gain_part, rate_part, bias_part
            else:
                tap_totals = tuple(
                    [a + b for a, b in zip(one, two)] for one, two in zip(tap_totals, parts)
                )
                gain_total = gain_total + gain_part
                rate_total = rate_total + rate_part
                bias_total = bias_total + bias_part
        for j in range(4):
            gtq_ref[j : j + 1, kc] = tap_totals[0][j]
            gtk_ref[j : j + 1, kc] = tap_totals[1][j]
            gtv_ref[j : j + 1, vc] = tap_totals[2][j]
        ggain_ref[0:1, :] = ggain_ref[0:1, :] + gain_total
        ghead_ref[0:1, :] = ghead_ref[0:1, :] + jnp.where(lane_row == head, rate_total, 0.0)
        ghead_ref[1:2, :] = ghead_ref[1:2, :] + jnp.where(lane_row == head, bias_total, 0.0)

    @pl.when(step == heads // per_step - 1)
    def _():
        first = key_cols + value_cols
        pre_a_ref[:, first : first + LANES] = gab_ref[...].astype(pre_a_ref.dtype)


HEADS_PER_STEP = 2


def mixer_specs(tokens, heads, key_size, value_size):
    per_step = HEADS_PER_STEP
    wide_key, wide_value = per_step * key_size, per_step * value_size
    key_first = heads * value_size // wide_key
    ab_first = (heads * value_size + heads * key_size) // LANES
    return [
        pl.BlockSpec((tokens, wide_key), lambda h: (0, key_first + h)),
        pl.BlockSpec((tokens, wide_key), lambda h: (0, key_first + h)),
        pl.BlockSpec((tokens, wide_value), lambda h: (0, h)),
        pl.BlockSpec((tokens, wide_value), lambda h: (0, h)),
        pl.BlockSpec((tokens, LANES), lambda h: (0, ab_first)),
        pl.BlockSpec((8, wide_key), lambda h: (0, h)),
        pl.BlockSpec((8, wide_key), lambda h: (0, h)),
        pl.BlockSpec((8, wide_value), lambda h: (0, h)),
        pl.BlockSpec((8, LANES), lambda h: (0, 0)),
        pl.BlockSpec((8, value_size), lambda h: (0, 0)),
    ]


def mixer_forward(pre_a, pre_b, small, length, heads, key_size, value_size):
    tokens = pre_a.shape[0]
    per_step = HEADS_PER_STEP
    return pl.pallas_call(
        functools.partial(mixer_forward_kernel, heads, length),
        grid=(heads // per_step,),
        in_specs=mixer_specs(tokens, heads, key_size, value_size),
        out_specs=[
            pl.BlockSpec((tokens, per_step * value_size), lambda h: (0, h)),
            pl.BlockSpec((per_step, tokens // length, length, length), lambda h: (h, 0, 0, 0)),
        ],
        out_shape=[
            jax.ShapeDtypeStruct((tokens, heads * value_size), BF16),
            jax.ShapeDtypeStruct((heads, tokens // length, length, length), F32),
        ],
        compiler_params=pltpu.CompilerParams(vmem_limit_bytes=VMEM_LIMIT),
        name="mixer_forward",
    )(pre_a, pre_b, pre_a, pre_b, pre_a, *small)


def mixer_backward(pre_a, pre_b, small, inverse, grad, length, heads, key_size, value_size):
    tokens, width_a = pre_a.shape
    width_b = pre_b.shape[1]
    per_step = HEADS_PER_STEP
    wide_key, wide_value = per_step * key_size, per_step * value_size
    fixed = lambda h: (0, 0)
    moving = lambda h: (0, h)
    return pl.pallas_call(
        functools.partial(mixer_backward_kernel, heads, length),
        grid=(heads // per_step,),
        in_specs=mixer_specs(tokens, heads, key_size, value_size)
        + [
            pl.BlockSpec((per_step, tokens // length, length, length), lambda h: (h, 0, 0, 0)),
            pl.BlockSpec((tokens, wide_value), moving),
        ],
        out_specs=[
            pl.BlockSpec((tokens, width_a), fixed),
            pl.BlockSpec((tokens, width_b), fixed),
            pl.BlockSpec((8, wide_key), moving),
            pl.BlockSpec((8, wide_key), moving),
            pl.BlockSpec((8, wide_value), moving),
            pl.BlockSpec((8, LANES), fixed),
            pl.BlockSpec((8, value_size), fixed),
        ],
        out_shape=[
            jax.ShapeDtypeStruct((tokens, width_a), BF16),
            jax.ShapeDtypeStruct((tokens, width_b), BF16),
            jax.ShapeDtypeStruct((8, heads * key_size), F32),
            jax.ShapeDtypeStruct((8, heads * key_size), F32),
            jax.ShapeDtypeStruct((8, heads * value_size), F32),
            jax.ShapeDtypeStruct((8, LANES), F32),
            jax.ShapeDtypeStruct((8, value_size), F32),
        ],
        scratch_shapes=[pltpu.VMEM((tokens, LANES), F32)],
        compiler_params=pltpu.CompilerParams(vmem_limit_bytes=VMEM_LIMIT),
        name="mixer_backward",
    )(pre_a, pre_b, pre_a, pre_b, pre_a, *small, inverse, grad)


def swapped(value):
    return lax.ppermute(value, "section", [(0, 1), (1, 0)])


def pair_sum(value):
    return value + swapped(value)


SIDE = 4


class Ring:
    def __init__(self, axis):
        if axis == "y":
            self.name, self.position = "rep", lax.axis_index("rep")
            self.pairs = lambda by: [(y, (y + by) % SIDE) for y in range(SIDE)]
            return
        self.name = "fsdp"
        index = lax.axis_index("fsdp")
        z, x = index // SIDE, index % SIDE
        if axis == "x":
            self.position = x
            step = lambda z, x, by: z * SIDE + (x + by) % SIDE
        else:
            self.position = z
            step = lambda z, x, by: (z + by) % SIDE * SIDE + x
        self.pairs = lambda by: [
            (z * SIDE + x, step(z, x, by)) for z in range(SIDE) for x in range(SIDE)
        ]

    def move(self, value, by):
        return lax.ppermute(value, self.name, self.pairs(by))


def ring_gather(block, ring):
    count = block.shape[0] // 2
    from_left = ring.move(block, 1)
    from_right = ring.move(block, -1)
    far_first = ring.move(from_left[:count], 1)
    far_last = ring.move(from_right[count:], -1)
    return block, from_right, far_first, far_last, from_left


def torus_gather(shard, x_first):
    rows = shard.shape[0]
    if x_first:
        block = jnp.concatenate(ring_gather(shard, Ring("x")), axis=0)
        pieces = ring_gather(block, Ring("z"))
        return jnp.concatenate(pieces, axis=0), pieces[1]
    block = jnp.concatenate(ring_gather(shard, Ring("z")), axis=0)
    own, right, far_first, far_last, left = ring_gather(block, Ring("x"))
    cut = lambda piece, k: piece[k * rows : (k + 1) * rows]
    rows_of = []
    for kz in range(SIDE):
        far = cut(far_first, kz) if kz < SIDE // 2 else cut(far_last, kz - SIDE // 2)
        rows_of += [cut(own, kz), cut(right, kz), far, cut(left, kz)]
    return jnp.concatenate(rows_of, axis=0), right


def added(first, *others):
    total = first.astype(F32)
    for other in others:
        total = total + other.astype(F32)
    return total.astype(BF16)


def ring_scatter(parts, ring):
    ahead, behind, rest, own = parts
    count = own.shape[0] // 2
    from_left = ring.move(ahead, 1)
    from_right = ring.move(behind, -1)
    next_left = ring.move(added(rest[:count], from_left[:count]), 1)
    next_right = ring.move(added(rest[count:], from_right[:count]), -1)
    return jnp.concatenate(
        [
            added(own[:count], next_left, from_right[count:]),
            added(own[count:], from_left[count:], next_right),
        ],
        axis=0,
    )


def scatter_parts(total, make):
    quarter, half = total // SIDE, total // SIDE // 2
    join = lambda one, two: make([(one, one + half), (two, two + half)])
    return [
        join(2 * quarter, quarter + half),
        join(2 * quarter + half, 3 * quarter),
        join(quarter, 3 * quarter + half),
        make([(0, quarter)]),
    ]


def torus_scatter(first_parts, x_first):
    first, second = ("x", "z") if x_first else ("z", "x")

    block = ring_scatter(first_parts, Ring(first))
    make = lambda cuts: jnp.concatenate([block[i:j] for i, j in cuts], axis=0)
    return ring_scatter(scatter_parts(block.shape[0], make), Ring(second))


class Chunks:
    def __init__(self, products):
        self.products = products
        self.parts = scatter_parts(products[0][0].shape[1], self.make)

    def make(self, cuts):
        blocks = []
        for left, right, extra in self.products:
            rows = jnp.concatenate([left[:, i:j] for i, j in cuts], axis=1)
            block = dot_tn(rows, right)
            if extra is not None:
                block = block + jnp.concatenate([extra[i:j] for i, j in cuts], axis=0)
            blocks.append(block.astype(BF16))
        return jnp.concatenate(blocks, axis=1)


def own_order(rows):
    index = lax.axis_index("fsdp")
    z, x = index // SIDE, index % SIDE
    place = jnp.arange(SIDE * SIDE * rows, dtype=jnp.int32)
    by_z, by_x, offset = place // (SIDE * rows), place // rows % SIDE, place % rows
    source = ((z + by_z) % SIDE * SIDE + (x + by_x) % SIDE) * rows + offset
    return (place[:, None] == source[None, :]).astype(BF16)


def flipped_order(rows):
    place = jnp.arange(SIDE * SIDE * rows, dtype=jnp.int32)
    by_x, by_z, offset = place // (SIDE * rows), place // rows % SIDE, place % rows
    source = (by_z * SIDE + by_x) * rows + offset
    return (place[:, None] == source[None, :]).astype(BF16)


def rep_sum(value):
    near = [(0, 1), (1, 0), (2, 3), (3, 2)]
    across = [(0, 3), (3, 0), (1, 2), (2, 1)]
    count = value.shape[0] // 2
    done = []
    for part, order in ((value[:count], (near, across)), (value[count:], (across, near))):
        for pairs in order:
            part = added(part, lax.ppermute(part, "rep", pairs))
        done.append(part)
    return jnp.concatenate(done, axis=0)


def dot(left, right):
    return jnp.dot(left, right, preferred_element_type=F32)


def dot_nt(left, right):
    return lax.dot_general(left, right, (((1,), (1,)), ((), ())), preferred_element_type=F32)


def dot_tn(left, right):
    return lax.dot_general(left, right, (((0,), (0,)), ((), ())), preferred_element_type=F32)


def inverse_rms(value):
    return lax.rsqrt(jnp.mean(value * value, axis=-1, keepdims=True) + 1e-06)


def norm_backward(value, gain, grad):
    scale = inverse_rms(value)
    unit = value * scale
    inner = grad * gain
    grad_value = scale * (inner - unit * jnp.mean(inner * unit, axis=-1, keepdims=True))
    return grad_value, jnp.sum(grad * unit, axis=0)


def per_device(
    inputs,
    out_grad,
    mixer_norm_gain,
    w_query,
    w_key,
    w_value,
    w_gate,
    w_alpha,
    w_beta,
    log_rate,
    dt_bias,
    conv_query,
    conv_key,
    conv_value,
    out_gain,
    w_out,
    gain_ffn,
    w_ffgate,
    w_ffup,
    w_ffdown,
):
    core = lax.axis_index("section")
    first_core = core == 0
    micro, _, length, width = inputs.shape
    tokens = micro * length
    members = lax.axis_size("fsdp")
    cores = 2
    all_heads = log_rate.shape[1]
    heads = all_heads // cores
    key_size = w_query.shape[2] // all_heads
    value_size = w_value.shape[2] // all_heads
    key_cols, value_cols = heads * key_size, heads * value_size
    ffn_cols = w_ffgate.shape[2] // cores
    rows = w_query.shape[1]
    taps = conv_query.shape[1]
    out_rows, down_rows = w_out.shape[1], w_ffdown.shape[1]
    value_split = conv_value.shape[2] // rows
    gain_rows = out_gain.shape[1]

    def choose(first, second):
        return jnp.where(first_core, first, second)

    small_cols = jnp.concatenate(
        [
            mixer_norm_gain[0][:, None],
            gain_ffn[0][:, None],
            conv_query[0].T,
            conv_key[0].T,
            conv_value[0].reshape(taps * value_split, rows).T,
            jnp.pad(out_gain[0], (0, rows - gain_rows))[:, None],
        ],
        axis=1,
    )
    small_count = small_cols.shape[1]
    ab_cols = 2 * heads
    spare = PAD - ab_cols - small_count
    main_a = value_cols + key_cols
    split = 2 * LANES
    out_first, down_first = ffn_cols, ffn_cols + value_cols

    lane_rows = out_rows + down_rows
    both_t = jnp.concatenate([w_out[0].T, w_ffdown[0].T], axis=1)
    both_t = jnp.pad(both_t, ((0, 0), (0, -lane_rows % LANES))).reshape(members, rows, -1)
    both_t = lax.all_to_all(both_t, "fsdp", split_axis=0, concat_axis=0, tiled=True)
    out_t = both_t[:, :, :out_rows].transpose(1, 0, 2).reshape(rows, members * out_rows)
    down_t = both_t[:, :, out_rows:lane_rows].transpose(1, 0, 2).reshape(rows, members * down_rows)

    def cut(w, k):
        n = w.shape[1] // cores
        return w[:, k * n : (k + 1) * n]

    def in_piece(k):
        return jnp.concatenate(
            [cut(w[0], k) for w in (w_value, w_query, w_alpha, w_beta)]
            + [small_cols, jnp.zeros((rows, spare), BF16)]
            + [cut(w[0], k) for w in (w_gate, w_key)],
            axis=1,
        )

    def ffn_piece(k):
        down = cut(down_t, k)
        return jnp.concatenate(
            [cut(w_ffgate[0], k), cut(out_t, k), down[:, :split], cut(w_ffup[0], k), down[:, split:]], axis=1
        )

    def both(make):
        left, right = make(0), make(1)
        own, sent = choose(left, right), choose(right, left)
        received = swapped(sent)
        return choose(own, received), choose(received, own)

    in_pieces = both(in_piece)
    ffn_pieces = both(ffn_piece)
    in_a = main_a + PAD
    ffn_a = down_first + split
    rate_rows = jnp.stack([log_rate[0], dt_bias[0]])
    other_rates = swapped(rate_rows)
    rates = (choose(rate_rows, other_rates), choose(other_rates, rate_rows))
    order = own_order(rows)
    flip = flipped_order(rows)

    def ordered(value):
        return dot(value, order)

    def unordered(value):
        high = value.astype(BF16)
        rest = value - high.astype(F32)
        middle = rest.astype(BF16)
        low = (rest - middle.astype(F32)).astype(BF16)
        return dot_nt(high, order) + (dot_nt(middle, order) + dot_nt(low, order))

    def flipped(value):
        return dot(value, flip).astype(BF16)

    def after(value, token):
        return value if token is None else lax.optimization_barrier((value, token))[0]

    def fetch(pieces, wide, token):
        pieces = after(pieces, token)
        full_a, token_a = torus_gather(pieces[:, :wide], True)
        full_b, token_b = torus_gather(pieces[:, wide:], False)
        return full_a, full_b, (token_a, token_b)

    def small_params(in_full, layer):
        first = main_a + ab_cols
        small_own = in_full[:, first : first + small_count].T
        small = small_own.astype(F32) if layer else dot_nt(small_own, order)
        at = 2
        conv_q = small[at : at + taps]
        conv_k = small[at + taps : at + 2 * taps]
        at += 2 * taps
        conv_v = small[at : at + taps * value_split].reshape(taps, value_split, members, rows)
        conv_v = conv_v.transpose(0, 2, 1, 3).reshape(taps, members * value_split * rows)
        at += taps * value_split
        gain_out = small[at].reshape(members, rows)[:, :gain_rows].reshape(1, members * gain_rows)

        def own_cols(value, count):
            mine = choose(value[:, :count], value[:, count:])
            return jnp.pad(mine, ((0, 8 - value.shape[0]), (0, 0)))

        rate = own_cols(rates[layer], heads)
        smalls = (
            own_cols(conv_q, key_cols),
            own_cols(conv_k, key_cols),
            own_cols(conv_v, value_cols),
            jnp.pad(rate, ((0, 0), (0, LANES - heads))),
            jnp.pad(gain_out, ((0, 7), (0, 0))),
        )
        return small_own[0].astype(F32), small_own[1].astype(F32), smalls

    def forward_layer(source, in_full, ffn_full, params):
        in_w, in_v = in_full
        ffn_w, ffn_v = ffn_full
        gain_mix, gain_in, smalls = params
        normed = (source * inverse_rms(source) * gain_mix).astype(BF16)
        pre_a, pre_b = dot(normed, in_w), dot(normed, in_v)
        mixed, inverse = mixer_forward(pre_a, pre_b, smalls, length, heads, key_size, value_size)
        after_mix = source + pair_sum(dot_nt(mixed, ffn_w[:, out_first:down_first]))
        normed_ffn = (after_mix * inverse_rms(after_mix) * gain_in).astype(BF16)
        gate_act = dot(normed_ffn, ffn_w[:, :ffn_cols])
        up_act = dot(normed_ffn, ffn_v[:, :ffn_cols])
        hidden = (gate_act * jax.nn.sigmoid(gate_act) * up_act).astype(BF16)
        part = dot_nt(hidden[:, :split], ffn_w[:, down_first:]) + dot_nt(hidden[:, split:], ffn_v[:, ffn_cols:])
        layer_out = after_mix + pair_sum(part)
        return layer_out, (source, normed, pre_a, pre_b, inverse, mixed, after_mix, normed_ffn, gate_act, up_act, hidden)

    def side_by_side(blocks):
        return jnp.concatenate([block.astype(BF16) for block in blocks], axis=1)

    def scattered(full):
        return lax.psum_scatter(full, "fsdp", scatter_dimension=0, tiled=True)

    def backward_layer(grad_top, saved, in_full, ffn_full, params, by_ring):
        source, normed, pre_a, pre_b, inverse, mixed, after_mix, normed_ffn, gate_act, up_act, hidden = saved
        in_w, in_v = in_full
        ffn_w, ffn_v = ffn_full
        gain_mix, gain_in, smalls = params
        down_grad = grad_top.astype(BF16)
        hidden_grad = jnp.concatenate(
            [dot(down_grad, ffn_w[:, down_first:]), dot(down_grad, ffn_v[:, ffn_cols:])], axis=1
        )
        gate_sig = jax.nn.sigmoid(gate_act)
        gate_grad = (hidden_grad * up_act * silu_slope(gate_act, gate_sig)).astype(BF16)
        up_grad = (hidden_grad * (gate_act * gate_sig)).astype(BF16)
        ffn_in_grad = pair_sum(dot_nt(gate_grad, ffn_w[:, :ffn_cols]) + dot_nt(up_grad, ffn_v[:, :ffn_cols]))
        residual, grad_gain_ffn = norm_backward(after_mix, gain_in, ffn_in_grad)
        mix_grad = grad_top + residual
        mix_low = mix_grad.astype(BF16)
        mixed_grad = dot(mix_low, ffn_w[:, out_first:down_first])
        if by_ring:
            parts_a = Chunks(
                [
                    (flipped(normed_ffn), gate_grad, None),
                    (flipped(mix_low), mixed, None),
                    (flipped(down_grad), hidden[:, :split], None),
                ]
            ).parts
            parts_b = Chunks([(normed_ffn, up_grad, None), (down_grad, hidden[:, split:], None)]).parts
            mixed_grad, parts_a, parts_b = lax.optimization_barrier((mixed_grad, parts_a, parts_b))
            grad_ffn = jnp.concatenate([torus_scatter(parts_a, True), torus_scatter(parts_b, False)], axis=1)
        else:
            full = side_by_side(
                [
                    dot_tn(normed_ffn, gate_grad),
                    dot_tn(mix_low, mixed),
                    dot_tn(down_grad, hidden[:, :split]),
                    dot_tn(normed_ffn, up_grad),
                    dot_tn(down_grad, hidden[:, split:]),
                ]
            )
            mixed_grad, full = lax.optimization_barrier((mixed_grad, full))
            grad_ffn = scattered(full)
        grad_ffn = rep_sum(grad_ffn)
        pre_a_grad, pre_b_grad, gtq, gtk, gtv, ghead, ggain = mixer_backward(
            pre_a, pre_b, smalls, inverse, mixed_grad, length, heads, key_size, value_size
        )
        normed_grad = pair_sum(dot_nt(pre_a_grad, in_w) + dot_nt(pre_b_grad, in_v))
        source_part, grad_gain_mix = norm_backward(source, gain_mix, normed_grad)
        source_grad = mix_grad + source_part

        def whole_cols(value):
            zeros = jnp.zeros_like(value)
            return choose(
                jnp.concatenate([value, zeros], axis=1), jnp.concatenate([zeros, value], axis=1)
            )

        conv_v = whole_cols(gtv[:taps]).reshape(taps, members, value_split, rows)
        conv_v = conv_v.transpose(0, 2, 1, 3).reshape(taps * value_split, members * rows)
        gain_out = ggain[0].reshape(members, gain_rows)
        head_part = whole_cols(ghead[:2, :heads]).reshape(1, 2 * all_heads)
        head_part = jnp.broadcast_to(head_part, (members, 2 * all_heads))
        tail = jnp.concatenate(
            [gain_out, head_part, jnp.zeros((members, rows - gain_rows - 2 * all_heads), F32)], axis=1
        )
        once = first_core.astype(F32)
        gains = jnp.stack([grad_gain_mix, grad_gain_ffn]) * once
        others = jnp.concatenate(
            [whole_cols(gtq[:taps]), whole_cols(gtk[:taps]), conv_v, tail.reshape(1, members * rows)], axis=0
        )
        others = others.astype(BF16)
        others = ordered(others).astype(BF16) if by_ring else others
        small = jnp.concatenate([gains.astype(BF16), others], axis=0)
        small = jnp.concatenate(
            [jnp.zeros((ab_cols, width), BF16), small, jnp.zeros((spare, width), BF16)], axis=0
        )
        if by_ring:
            small = lax.dot_general(flip, small, (((0,), (1,)), ((), ())), preferred_element_type=F32)
            turned = flipped(normed)
            grad_in = (
                torus_scatter(
                    Chunks([(turned, pre_a_grad[:, :main_a], None), (turned, pre_a_grad[:, main_a:], small)]).parts,
                    True,
                ),
                torus_scatter(Chunks([(normed, pre_b_grad, None)]).parts, False),
            )
            grad_in = jnp.concatenate(grad_in, axis=1)
        else:
            full = side_by_side(
                [
                    dot_tn(normed, pre_a_grad[:, :main_a]),
                    dot_tn(normed, pre_a_grad[:, main_a:]) + small.T.astype(F32),
                    dot_tn(normed, pre_b_grad),
                ]
            )
            source_grad, full = lax.optimization_barrier((source_grad, full))
            grad_in = scattered(full)
        grad_in = rep_sum(grad_in)
        return source_grad, grad_in, grad_ffn

    def to_owner(first, second):
        own = choose(first, second)
        received = swapped(choose(second, first))
        return choose(own, received), choose(received, own)

    source = ordered(inputs.reshape(tokens, width))
    in_0a, in_0b, token = fetch(in_pieces[0], in_a, None)
    ffn_0a, ffn_0b, token = fetch(ffn_pieces[0], ffn_a, token)
    in_1 = lax.all_gather(in_pieces[1], "fsdp", axis=0, tiled=True)
    ffn_1 = lax.all_gather(ffn_pieces[1], "fsdp", axis=0, tiled=True)
    in_0, ffn_0 = (in_0a, in_0b), (ffn_0a, ffn_0b)
    in_1, ffn_1 = (in_1[:, :in_a], in_1[:, in_a:]), (ffn_1[:, :ffn_a], ffn_1[:, ffn_a:])
    params_0, params_1 = small_params(in_0a, 0), small_params(in_1[0], 1)
    first_out, first_saved = forward_layer(source, in_0, ffn_0, params_0)
    middle = dot_nt(first_out.astype(BF16), order)
    block_out, second_saved = forward_layer(middle, in_1, ffn_1, params_1)
    cotangent = out_grad.reshape(tokens, width).astype(F32)
    second_grad, second_in, second_ffn = backward_layer(cotangent, second_saved, in_1, ffn_1, params_1, False)
    input_grad, first_in, first_ffn = backward_layer(
        ordered(second_grad.astype(BF16)), first_saved, in_0, ffn_0, params_0, True
    )
    in_left, in_right = to_owner(first_in, second_in)
    ffn_left, ffn_right = to_owner(first_ffn, second_ffn)

    def joined(left, right, first, count):
        span = slice(first, first + count)
        return jnp.concatenate([left[:, span], right[:, span]], axis=1).astype(F32)[None]

    gate_first = main_a + PAD
    up_first = down_first + split
    down_rest = up_first + ffn_cols
    full_out = jnp.concatenate(
        [side[:, out_first:down_first] for side in (ffn_left, ffn_right)], axis=1
    ).reshape(rows, members, out_rows)
    full_down = jnp.concatenate(
        [part for side in (ffn_left, ffn_right) for part in (side[:, down_first:up_first], side[:, down_rest:])], axis=1
    ).reshape(rows, members, down_rows)
    back = jnp.concatenate([full_out, full_down], axis=2).transpose(1, 0, 2)
    back = jnp.pad(back, ((0, 0), (0, 0), (0, -lane_rows % LANES)))
    back = lax.all_to_all(back, "fsdp", split_axis=0, concat_axis=0, tiled=True).reshape(width, -1)
    grad_out = back[:, :out_rows].T.astype(F32)
    grad_down = back[:, out_rows:lane_rows].T.astype(F32)

    first = main_a + ab_cols
    small = in_left[:, first : first + small_count].astype(F32) + in_right[:, first : first + small_count].astype(F32)
    small = small.T
    tail = small[small_count - 1]
    conv_at = 2 + 2 * taps
    head_grads = tail[gain_rows : gain_rows + 2 * all_heads].reshape(2, all_heads)
    edges = choose(unordered(input_grad), block_out).reshape(1, micro, 1, length, width)
    return (
        edges,
        small[0][None],
        joined(in_left, in_right, value_cols, key_cols),
        joined(in_left, in_right, gate_first + value_cols, key_cols),
        joined(in_left, in_right, 0, value_cols),
        joined(in_left, in_right, gate_first, value_cols),
        joined(in_left, in_right, main_a, heads),
        joined(in_left, in_right, main_a + heads, heads),
        head_grads[0:1],
        head_grads[1:2],
        small[2 : 2 + taps][None],
        small[2 + taps : 2 + 2 * taps][None],
        small[conv_at : conv_at + taps * value_split].reshape(1, taps, value_split * rows),
        tail[:gain_rows][None],
        grad_out[None],
        small[1][None],
        joined(ffn_left, ffn_right, 0, ffn_cols),
        joined(ffn_left, ffn_right, up_first, ffn_cols),
        grad_down[None],
    )


def solution(mesh):
    across = P("section", "fsdp", None)
    lanes = P("section", None, "fsdp")
    vector = P("section", "fsdp")
    rates = P("section", None)
    tokens = P(None, ("rep", "fsdp"), None, None)
    placed = (
        (tokens, tokens, vector)
        + (across,) * 6
        + (rates, rates, lanes, lanes, lanes, vector, across, vector, across, across, across)
    )
    return jax.shard_map(
        per_device,
        mesh=mesh,
        in_specs=placed,
        out_specs=(P("section", None, ("rep", "fsdp"), None, None), vector)
        + (across,) * 6
        + (rates, rates, lanes, lanes, lanes, vector, across, vector, across, across, across),
        check_vma=False,
    )
```
